32 devices in a mesh: dp: 2 (over x), expert: 16 (over z, y, core).
Axes of the slice: x: 2, y: 2, z: 4, core: 2. Of those that a mesh axis runs over, the one named last changes fastest.
Arguments:
- tokens: bfloat16 [256, 4096], P('dp', 'expert'), may hold values from -6 to 6
- norm_gain: float32 [4096], replicated, may hold values from 0.1 to 1.9
- routes: int32 [256, 2], P('dp'), may hold values from 0 to 15, all different within a row; in each aligned block of 128 rows (0 to 127, 128 to 255, ...) at most 20 rows name the same one
- route_prob: float32 [256, 2], P('dp'), may hold values from 0.2 to 1
- gate_weight: bfloat16 [16, 4096, 256], P('expert', None, 'dp'), may hold values from -0.09375 to 0.09375
- up_weight: bfloat16 [16, 4096, 256], P('expert', None, 'dp'), may hold values from -0.09375 to 0.09375
- down_weight: bfloat16 [16, 256, 4096], P('expert', 'dp'), may hold values from -0.375 to 0.375
- key_value_weight: bfloat16 [4096, 2048], P('expert'), may hold values from -0.09375 to 0.09375
- key_value_target: bfloat16 [256, 2048], P('dp', 'expert'), may hold values from -6 to 6
- concept_mask: int32 [256], P('dp'), may hold values 0 or 1
Outputs:
- down_grad: bfloat16 [16, 256, 4096], P('expert', 'dp')
- key_value_grad: float32 [4096, 2048], P('expert', 'dp')
The draws below stay inside these ranges and needn't reach their ends.
Inputs may be any that keep to these rules, and one draw needn't show every extreme that they name: `routes`: in each aligned block of 128 rows no expert is named by more than 20 rows; the two choices of a token differ.
All inputs are finite; a program needn't handle non-finite values. No bound on the sum of `concept_mask` on one device may be relied on, other than what follows from the above.
Results may differ from the reference program's by a relative error of at most 0.033.
Values may be sent and summed in bfloat16 or wider, within the bound.
A program may use at most 64 MiB of HBM per device.

```python
import math
import jax
import jax.numpy as jnp
import numpy as np
from jax import lax

D = 4096
KV = 1024
FF_DEV = 128
TOP = 2
TOK = 128
FF = 256
EXPERTS = 16
CAP = 20
TOKENS = 256
N_DP = 2
N_EXPERT = 16


def place_ends(entries, own_key, smallest, high):
    longest = entries.shape.index(max(entries.shape))
    spots = []
    for shift in (0, 1):
        where = [jax.random.randint(jax.random.fold_in(own_key, axis), (), 0, length) for axis, length in enumerate(entries.shape)]
        where[longest] = (where[longest] + shift) % entries.shape[longest]
        spots.append(tuple(where))
    return entries.at[spots[0]].set(smallest).at[spots[1]].set(high)


def block_levels(own_key, dims, cuts, smallest, top_value):
    loudness = 1.0
    for dim, shards_of in cuts:
        steps = jax.random.uniform(jax.random.fold_in(jax.random.fold_in(own_key, 6), dim), (shards_of,), jnp.float32, smallest / len(cuts), top_value / len(cuts))
        loudness = loudness * jnp.repeat(jnp.exp(steps), dims[dim] // shards_of).reshape((-1,) + (1,) * (len(dims) - 1 - dim))
    return loudness


def assign_block(rng, own, number, rows, number_of, top, limit, slope):
    ranking = jax.random.permutation(rng, number_of)
    heavy_load, usual = shares(number_of, rows * top, limit, slope, True), shares(number_of, rows * top, limit, slope, False)
    places = jnp.arange(number_of)

    def named(lengths, turn):
        used = int((lengths > 0).sum())
        fixed = max(1, used // 4)
        moved = fixed + (places - fixed + turn * (used - fixed)) % max(1, number_of - fixed)
        return jnp.zeros((number_of,), jnp.int32).at[ranking[jnp.where(places < fixed, places, moved)]].set(jnp.asarray(lengths, jnp.int32))

    lengths = jnp.where(number % 4 == 0, named(heavy_load, number // 4), named(usual, number - number // 4 - 1))
    mixed = jax.random.permutation(jax.random.fold_in(own, 3), number_of)
    giver, receiver = mixed[0:number_of // 2 * 2:2], mixed[1:number_of // 2 * 2:2]
    room = jnp.minimum(lengths[giver] - 1, limit - lengths[receiver]) // 2
    room = jnp.where((giver == ranking[0]) | (receiver == ranking[0]) | (lengths[receiver] == 0), 0, jnp.maximum(room, 0))
    moved = jax.random.randint(jax.random.fold_in(own, 4), (number_of // 2,), 0, 1 << 20) % (room + 1)
    lengths = lengths.at[giver].add(-moved).at[receiver].add(moved)
    members = jnp.searchsorted(jnp.cumsum(lengths), jnp.arange(rows * top), side="right").astype(jnp.int32)
    table = members.reshape(top, rows).T
    table = table[jax.random.permutation(jax.random.fold_in(own, 1), rows)]
    turn = jax.random.randint(jax.random.fold_in(own, 2), (rows, 1), 0, top)
    return jnp.take_along_axis(table, (jnp.arange(top)[None, :] + turn) % top, axis=1)


def shares(number_of, total, most, lean, full):
    portions = [(1 << 20) // math.isqrt(grade ** lean) + 1 for grade in range(1, number_of + 1)]
    largest = most if full else min(most, max(-(-total // number_of), total * portions[0] // sum(portions)))
    least = 1 if total - largest >= number_of - 1 else 0
    given, surplus = [largest] + [least] * (number_of - 1), total - largest - least * (number_of - 1)
    while surplus > 0:
        candidates = [i for i in range(1, number_of) if given[i] < largest] or [i for i in range(1, number_of) if given[i] < most]
        pool, left = sum([portions[i] for i in candidates]), surplus
        for i in candidates:
            more = min(most - given[i], max(1, left * portions[i] // pool), surplus)
            given[i] = given[i] + more
            surplus = surplus - more
    return np.array(given)


def centred(key, dims, deviation, bound, cuts=(), held_as=jnp.bfloat16):
    entries = deviation * jax.random.normal(key, dims, jnp.float32)
    if cuts:
        entries = entries * block_levels(key, dims, cuts, -0.22, 0.18)
    return jnp.clip(entries, -bound, bound).astype(held_as)


def setup_inputs(seed: int = 0) -> dict:
    streams_of = jax.random.split(jax.random.key(seed), 11)
    tokens = centred(streams_of[0], (TOKENS, D), 1.0, 6.0, ((0, 2), (1, 16)))
    norm_gain = jnp.clip(1.0 + 0.18 * jax.random.normal(streams_of[1], (D,), jnp.float32), 0.1, 1.9)
    routes_keys = jax.random.split(jax.random.fold_in(streams_of[2], 1), TOKENS // TOK)
    routes_turns = jax.random.permutation(jax.random.fold_in(streams_of[2], 3), TOKENS // TOK)
    routes = jax.vmap(lambda own, number: assign_block(jax.random.fold_in(streams_of[2], 2), own, number, TOK, EXPERTS, TOP, CAP, 2))(routes_keys, routes_turns).reshape((TOKENS, TOP))
    route_prob = jnp.clip(0.2 + 0.8 * jax.random.uniform(streams_of[3], (TOKENS, TOP), jnp.float32) ** block_levels(streams_of[3], (TOKENS, TOP), ((0, 2),), -0.2, 0.2), 0.2, 1.0)
    gate_weight = centred(streams_of[4], (EXPERTS, D, FF), D ** -0.5, 0.09375, ((0, 16), (2, 2)))
    up_weight = centred(streams_of[5], (EXPERTS, D, FF), D ** -0.5, 0.09375, ((0, 16), (2, 2)))
    down_weight = centred(streams_of[6], (EXPERTS, FF, D), FF ** -0.5, 0.375, ((0, 16), (1, 2)))
    key_value_weight = centred(streams_of[7], (D, 2 * KV), D ** -0.5, 0.09375, ((0, 16),))
    key_value_target = centred(streams_of[8], (TOKENS, 2 * KV), 1.0, 6.0, ((0, 2), (1, 16)))
    concept_mask = place_ends((jax.random.randint(streams_of[9], (TOKENS,), 0, 2) < 1).astype(jnp.int32), jax.random.fold_in(streams_of[9], 1), 0, 1)
    return dict(tokens=tokens, norm_gain=norm_gain, routes=routes, route_prob=route_prob, gate_weight=gate_weight, up_weight=up_weight, down_weight=down_weight, key_value_weight=key_value_weight, key_value_target=key_value_target, concept_mask=concept_mask)


def slot_numbers(block_routes):
    flat = block_routes.reshape(-1)
    onehot = (flat[:, None] == jnp.arange(EXPERTS, dtype=jnp.int32)[None, :]).astype(jnp.int32)
    before = jnp.cumsum(onehot, axis=0) - onehot
    return (flat, lax.optimization_barrier(jnp.sum(before * onehot, axis=1)).astype(jnp.int32))

def reference(tokens, norm_gain, routes, route_prob, gate_weight, up_weight, down_weight, key_value_weight, key_value_target, concept_mask):
    slot_total = N_DP * CAP
    values = tokens.astype(jnp.float32)
    mean_sq = lax.optimization_barrier(jnp.mean(values * values, axis=1, keepdims=True))
    normed = (values * lax.rsqrt(mean_sq + 1e-06) * norm_gain[None, :]).astype(jnp.bfloat16)
    chosen, slot = jax.vmap(slot_numbers)(routes.reshape(N_DP, TOK, TOP))
    block_id = jnp.arange(N_DP, dtype=jnp.int32)[:, None]
    position = (chosen * slot_total + block_id * CAP + slot).reshape(-1).astype(jnp.int32)
    token_of = (jnp.arange(TOKENS * TOP, dtype=jnp.int32) // TOP).astype(jnp.int32)
    slot_rows = jnp.zeros((EXPERTS * slot_total, D), jnp.bfloat16).at[position].set(normed[token_of])
    slot_rows = slot_rows.reshape(EXPERTS, slot_total, D)

    def expert_forward(group):
        rows_in, gate_mat, up_mat, down_mat = group
        gate_val = jnp.dot(rows_in, gate_mat, preferred_element_type=jnp.float32)
        up_val = jnp.dot(rows_in, up_mat, preferred_element_type=jnp.float32)
        hidden = (jax.nn.silu(gate_val) * up_val).astype(jnp.bfloat16)
        pieces = jnp.einsum('rjf,jfd->jrd', hidden.reshape(slot_total, N_DP, FF_DEV).astype(jnp.float32), down_mat.reshape(N_DP, FF_DEV, D).astype(jnp.float32))
        rounded = lax.optimization_barrier(pieces.astype(jnp.bfloat16))
        return (hidden, lax.optimization_barrier(jnp.sum(rounded.astype(jnp.float32), axis=0)).astype(jnp.bfloat16))
    hidden_all, expert_out = lax.map(expert_forward, (slot_rows, gate_weight, up_weight, down_weight))
    prob_flat = route_prob.reshape(-1)
    picked = expert_out.reshape(EXPERTS * slot_total, D)[position].astype(jnp.float32) * prob_flat[:, None]
    expert_mix = picked.reshape(TOKENS, TOP, D).sum(axis=1)
    state = (values + expert_mix).astype(jnp.bfloat16)
    width = D // N_EXPERT
    state_blocks = state.reshape(TOKENS, N_EXPERT, width).transpose(1, 0, 2)
    weight_blocks = key_value_weight.reshape(N_EXPERT, width, 2 * KV)

    def add_block(total, group):
        piece = jnp.dot(group[0], group[1], preferred_element_type=jnp.float32).astype(jnp.bfloat16)
        piece = lax.optimization_barrier(piece)
        return (total + piece.astype(jnp.float32), None)
    key_value, unused = lax.scan(add_block, jnp.zeros((TOKENS, 2 * KV), jnp.float32), (state_blocks, weight_blocks))
    mask_col = concept_mask.astype(jnp.float32)[:, None]
    cotangent = (mask_col * (key_value - key_value_target.astype(jnp.float32)) * TOK ** (-0.5)).astype(jnp.bfloat16)

    def add_grad(total, group):
        piece = jnp.dot(group[0].T, group[1], preferred_element_type=jnp.float32).astype(jnp.bfloat16)
        piece = lax.optimization_barrier(piece)
        return (total + piece.astype(jnp.float32), None)
    key_value_grad, unused2 = lax.scan(add_grad, jnp.zeros((D, 2 * KV), jnp.float32), (state.reshape(N_DP, TOK, D), cotangent.reshape(N_DP, TOK, 2 * KV)))
    state_grad = jnp.dot(cotangent, key_value_weight.T, preferred_element_type=jnp.float32)
    row_grad = (state_grad[token_of] * prob_flat[:, None]).astype(jnp.bfloat16)
    slot_grad = jnp.zeros((EXPERTS * slot_total, D), jnp.bfloat16).at[position].set(row_grad)
    slot_grad = slot_grad.reshape(EXPERTS, slot_total, D)

    def expert_grad(group):
        return jnp.dot(group[0].T, group[1], preferred_element_type=jnp.float32).astype(jnp.bfloat16)
    down_grad = lax.map(expert_grad, (hidden_all, slot_grad))
    return (down_grad, key_value_grad)
```

```python
import functools

import jax
import jax.numpy as jnp
from jax import lax
from jax.experimental import pallas as pl
from jax.experimental.pallas import tpu as pltpu
from jax.sharding import PartitionSpec as P

eps_norm = 1e-06
f32, bf16 = jnp.float32, jnp.bfloat16


def dot(a, b, contract):
    return lax.dot_general(a, b, ((contract[:1], contract[1:]), ((), ())), preferred_element_type=f32)


def kernel(
    dp_count,
    expert_count,
    capacity,
    tokens_ref,
    gain_ref,
    routes_ref,
    routes_row_ref,
    prob_ref,
    prob_row_ref,
    mask_ref,
    target_ref,
    gate_hbm,
    up_hbm,
    down_hbm,
    kvw_hbm,
    down_grad_ref,
    kv_grad_ref,
    gate,
    up,
    down,
    kvw,
    kvw_t,
    place,
    rows_out,
    rows_in,
    hidden_ref,
    part_out,
    part_in,
    proj_out,
    proj_in,
    cot,
    cot_swap,
    state_t,
    grad_out,
    grad_in,
    load_sem,
    send_sem,
    recv_sem,
):
    device_count = dp_count * expert_count
    slots, width = rows_out.shape[1:]
    token_rows = tokens_ref.shape[0]
    model_width = width * expert_count
    me_dp, me_expert = lax.axis_index("dp"), lax.axis_index("expert")
    me = me_dp * expert_count + me_expert

    loads = [
        pltpu.make_async_copy(src, dst, load_sem.at[i])
        for i, (src, dst) in enumerate([(kvw_hbm, kvw), (gate_hbm, gate), (up_hbm, up), (down_hbm, down)])
    ]
    for load in loads:
        load.start()

    def place_of(number):
        return lax.div(number, expert_count), lax.rem(number, expert_count)

    barrier = pltpu.get_barrier_semaphore()

    def greet(step, carry):
        pl.semaphore_signal(
            barrier,
            inc=1,
            device_id=place_of(lax.rem(me + step, device_count)),
            device_id_type=pl.DeviceIdType.MESH,
        )
        return carry

    lax.fori_loop(1, device_count, greet, 0)

    def remote(src, dst, phase, target):
        return pltpu.make_async_remote_copy(
            src_ref=src,
            dst_ref=dst,
            send_sem=send_sem.at[phase],
            recv_sem=recv_sem.at[phase],
            device_id=target,
            device_id_type=pl.DeviceIdType.MESH,
        )

    def to_all(phase, source, landing):
        def step_to(step, carry):
            other = lax.rem(me + step, device_count)
            remote(source(other), landing.at[me], phase, place_of(other)).start()
            return carry

        lax.fori_loop(1, device_count, step_to, 0)

    def to_expert(phase, source, landing):
        def step_to(step, carry):
            other = lax.rem(me_expert + step, expert_count)
            remote(source(other), landing.at[me_expert], phase, (me_dp, other)).start()
            return carry

        lax.fori_loop(1, expert_count, step_to, 0)

    def to_dp(phase, source, landing):
        def step_to(step, carry):
            other = lax.rem(me_dp + step, dp_count)
            remote(source(other), landing.at[me_dp], phase, (other, me_expert)).start()
            return carry

        lax.fori_loop(1, dp_count, step_to, 0)

    def arrived(phase, landing):
        most = landing.at[pl.ds(0, landing.shape[0] - 1)]
        pltpu.make_async_copy(most, most, recv_sem.at[phase]).wait()

    def sent(phase, landing):
        most = landing.at[pl.ds(0, landing.shape[0] - 1)]
        pltpu.make_async_copy(most, most, send_sem.at[phase]).wait()

    slot_count = expert_count * slots
    older = lax.broadcasted_iota(jnp.int32, (token_rows, token_rows), 0)
    newer = lax.broadcasted_iota(jnp.int32, (token_rows, token_rows), 1)
    before = (older < newer).astype(f32).astype(bf16)
    after = (older > newer).astype(f32).astype(bf16)

    names_row = lax.broadcasted_iota(jnp.int32, (expert_count, token_rows), 0)
    picks_row = [(names_row == routes_row_ref[k : k + 1, :]).astype(f32) for k in range(2)]
    counts_row = dot((picks_row[0] + picks_row[1]).astype(bf16), before, (1, 0))
    number_row = lax.broadcasted_iota(jnp.int32, (slot_count, token_rows), 0)
    total = None
    for k in range(2):
        slot = jnp.sum(picks_row[k] * counts_row, axis=0, keepdims=True).astype(jnp.int32)
        chosen = (number_row == routes_row_ref[k : k + 1, :] * slots + slot).astype(f32)
        place[k] = chosen.astype(bf16)
        total = chosen if total is None else total + chosen
    rows_out[...] = (
        dot(total.astype(bf16), tokens_ref[...], (1, 0)).astype(bf16).reshape(expert_count, slots, width)
    )
    pl.semaphore_wait(barrier, device_count - 1)
    to_all(0, lambda other: rows_out.at[lax.rem(other, expert_count)], rows_in)
    rows_in[me] = rows_out[me_expert]

    loads[0].wait()
    kvw_t[...] = kvw[...].T
    names = lax.broadcasted_iota(jnp.int32, (token_rows, expert_count), 1)
    picks = [(names == routes_ref[:, k : k + 1]).astype(f32) for k in range(2)]
    counts = dot(after, (picks[0] + picks[1]).astype(bf16), (1, 0))
    number = lax.broadcasted_iota(jnp.int32, (token_rows, slot_count), 1)
    gather = []
    for k in range(2):
        slot = jnp.sum(picks[k] * counts, axis=1, keepdims=True).astype(jnp.int32)
        gather.append((number == routes_ref[:, k : k + 1] * slots + slot).astype(f32).astype(bf16))
    for load in loads[1:]:
        load.wait()
    arrived(0, rows_in)

    all_rows = dp_count * slots
    squares = jnp.zeros((all_rows, 1), f32)

    def features(ref, block):
        pieces = [ref[b * expert_count + block] for b in range(dp_count)]
        return jnp.concatenate(pieces, axis=0)

    for f in range(expert_count):
        piece = features(rows_in, f).astype(f32)
        squares = squares + jnp.sum(piece * piece, axis=1, keepdims=True)
    scale = lax.rsqrt(squares / model_width + eps_norm)
    gate_val = jnp.zeros((all_rows, gate.shape[1]), f32)
    up_val = jnp.zeros((all_rows, gate.shape[1]), f32)
    for f in range(expert_count):
        span = pl.ds(f * width, width)
        normed = (features(rows_in, f).astype(f32) * scale * gain_ref[:, span]).astype(bf16)
        gate_val = gate_val + dot(normed, gate[span, :], (1, 0))
        up_val = up_val + dot(normed, up[span, :], (1, 0))
    hidden = (gate_val / (1.0 + jnp.exp(-gate_val)) * up_val).astype(bf16)
    hidden_ref[...] = hidden
    for f in range(expert_count):
        piece = dot(hidden, down[:, pl.ds(f * width, width)], (1, 0)).astype(bf16)
        for b in range(dp_count):
            part_out[b * expert_count + f] = piece[b * slots : (b + 1) * slots]
    to_all(1, lambda other: part_out.at[other], part_in)
    part_in[me] = part_out[me]
    arrived(1, part_in)

    expert_out = part_in[pl.ds(0, expert_count)].astype(f32)
    for b in range(1, dp_count):
        expert_out = expert_out + part_in[pl.ds(b * expert_count, expert_count)].astype(f32)
    expert_out = expert_out.astype(bf16).reshape(slot_count, width)
    state = tokens_ref[...].astype(f32)
    for k in range(2):
        state = state + prob_ref[:, k : k + 1] * dot(gather[k], expert_out, (1, 0))
    state = state.astype(bf16)

    proj = dot(kvw_t[...], state, (1, 1)).astype(bf16)
    proj_out[...] = proj.reshape(proj_out.shape)
    to_expert(2, lambda other: proj_out.at[other], proj_in)
    proj_in[me_expert] = proj_out[me_expert]
    state_t[me_dp] = state.astype(f32).T.astype(bf16)
    to_dp(3, lambda other: state_t.at[me_dp], state_t)
    arrived(2, proj_in)
    key_value = jnp.sum(proj_in[...].astype(f32), axis=0)
    cot[me_expert] = (
        mask_ref[...].astype(f32) * (key_value - target_ref[...].astype(f32)) * token_rows ** (-0.5)
    ).astype(bf16)
    to_expert(4, lambda other: cot.at[me_expert], cot)
    arrived(4, cot)

    share = expert_count // dp_count
    to_dp(5, lambda other: cot.at[pl.ds(other * share, share)], cot_swap)
    cot_swap[me_dp] = cot[pl.ds(me_dp * share, share)]
    cot_all = cot[...].reshape(kvw.shape[1], token_rows)
    state_grad_t = dot(kvw[...], cot_all, (1, 0))
    grads = jnp.zeros((slot_count, width), f32)
    for k in range(2):
        pair_grad = (state_grad_t * prob_row_ref[k : k + 1, :]).astype(bf16)
        grads = grads + dot(place[k], pair_grad, (1, 1))
    grad_out[...] = grads.astype(bf16).reshape(expert_count, slots, width)
    to_all(6, lambda other: grad_out.at[lax.rem(other, expert_count)], grad_in)
    grad_in[me] = grad_out[me_expert]

    arrived(3, state_t)
    arrived(5, cot_swap)
    columns = kv_grad_ref.shape[1]
    kv_grad = jnp.zeros(kv_grad_ref.shape, f32)
    for b in range(dp_count):
        kv_grad = kv_grad + dot(state_t[b], cot_swap[b].reshape(columns, token_rows), (1, 1))
    kv_grad_ref[...] = kv_grad
    hidden_t = hidden_ref[...].astype(f32).T.astype(bf16)
    arrived(6, grad_in)
    for f in range(expert_count):
        down_grad_ref[:, pl.ds(f * width, width)] = dot(hidden_t, features(grad_in, f), (1, 0)).astype(bf16)

    for phase, landing in enumerate([rows_in, part_in, proj_in, state_t, cot, cot_swap, grad_in]):
        sent(phase, landing)


def per_device(
    tokens,
    norm_gain,
    routes,
    route_prob,
    gate_weight,
    up_weight,
    down_weight,
    key_value_weight,
    key_value_target,
    concept_mask,
):
    token_rows, width = tokens.shape
    dp_count, expert_count = lax.axis_size("dp"), lax.axis_size("expert")
    device_count = dp_count * expert_count
    capacity = 5 * token_rows * routes.shape[1] // (4 * expert_count)
    slots = -(-capacity // 16) * 16
    slot_count = expert_count * slots
    model_width, units = gate_weight.shape[1:]
    keys = key_value_weight.shape[1]
    own_keys = keys // expert_count
    in_vmem = pl.BlockSpec(memory_space=pltpu.VMEM)
    in_any = pl.BlockSpec(memory_space=pl.ANY)
    pieces = pltpu.VMEM((device_count, slots, width), bf16)
    own_pieces = pltpu.VMEM((expert_count, slots, width), bf16)
    key_pieces = pltpu.VMEM((expert_count, own_keys, token_rows), bf16)
    down_grad, kv_grad = pl.pallas_call(
        functools.partial(kernel, dp_count, expert_count, capacity),
        out_shape=(
            jax.ShapeDtypeStruct((units, model_width), bf16),
            jax.ShapeDtypeStruct((width, keys // dp_count), f32),
        ),
        in_specs=[in_vmem] * 8 + [in_any] * 4,
        out_specs=(in_vmem, in_vmem),
        scratch_shapes=[
            pltpu.VMEM((model_width, units), bf16),
            pltpu.VMEM((model_width, units), bf16),
            pltpu.VMEM((units, model_width), bf16),
            pltpu.VMEM((width, keys), bf16),
            pltpu.VMEM((keys, width), bf16),
            pltpu.VMEM((2, slot_count, token_rows), bf16),
            own_pieces,
            pieces,
            pltpu.VMEM((dp_count * slots, units), bf16),
            pieces,
            pieces,
            key_pieces,
            key_pieces,
            key_pieces,
            pltpu.VMEM((dp_count, expert_count // dp_count, own_keys, token_rows), bf16),
            pltpu.VMEM((dp_count, width, token_rows), bf16),
            own_pieces,
            pieces,
            pltpu.SemaphoreType.DMA((4,)),
            pltpu.SemaphoreType.DMA((7,)),
            pltpu.SemaphoreType.DMA((7,)),
        ],
        compiler_params=pltpu.CompilerParams(
            collective_id=0, has_side_effects=True, vmem_limit_bytes=48 * 1024 * 1024
        ),
    )(
        tokens,
        norm_gain[None, :],
        routes,
        routes.T,
        route_prob,
        route_prob.T,
        concept_mask[None, :],
        key_value_target.T,
        gate_weight[0],
        up_weight[0],
        down_weight[0],
        key_value_weight,
    )
    return (down_grad[None], kv_grad)


def solution(mesh):
    placed = (
        P("dp", "expert"),
        P(),
        P("dp", None),
        P("dp", None),
        P("expert", None, "dp"),
        P("expert", None, "dp"),
        P("expert", "dp", None),
        P("expert", None),
        P("dp", "expert"),
        P("dp"),
    )
    return jax.shard_map(
        per_device,
        mesh=mesh,
        in_specs=placed,
        out_specs=(P("expert", "dp", None), P("expert", "dp")),
        check_vma=False,
    )
```

```python
import functools

import jax
import jax.numpy as jnp
from jax import lax
from jax.experimental import pallas as pl
from jax.experimental.pallas import tpu as pltpu
from jax.sharding import PartitionSpec as P

eps_norm = 1e-06
f32, bf16 = jnp.float32, jnp.bfloat16


def dot(a, b, contract):
    return lax.dot_general(a, b, ((contract[:1], contract[1:]), ((), ())), preferred_element_type=f32)


def swapped(index, step):
    bit = 1
    while bit <= step:
        if step & bit:
            index = index + bit - 2 * bit * lax.rem(lax.div(index, bit), 2)
        bit *= 2
    return index


def sizes(dp_count, expert_count, token_rows, top_count, width):
    capacity = 5 * token_rows * top_count // (4 * expert_count)
    halves = width // 128
    return capacity, halves, -(-halves * capacity // 16) * 16


def sem_plan(dp_count, groups):
    plan, at = {}, 0
    for name, count in (
        ("rows", groups),
        ("rows_x", dp_count * groups),
        ("part_x", dp_count * groups),
        ("part", 1),
        ("proj_core", 2),
        ("proj_mid", groups),
        ("proj", 1),
        ("state", 1),
        ("cot", groups),
        ("cot_mid", groups),
        ("cot_core", 1),
        ("swap", 1),
        ("swap_core", 1),
        ("grad", groups),
        ("grad_x", dp_count * groups),
    ):
        plan[name] = at
        at += count
    return plan, at


def kernel(
    dp_count,
    expert_count,
    top_count,
    tokens_hbm,
    routes_hbm,
    prob_hbm,
    mask_hbm,
    gain_hbm,
    target_hbm,
    kvw_hbm,
    gate_hbm,
    up_hbm,
    down_hbm,
    down_grad_ref,
    kv_grad_ref,
    tokens_ref,
    routes_ref,
    prob_ref,
    mask_ref,
    gain_ref,
    target_ref,
    kvw,
    gate,
    up,
    down,
    kvw_t,
    place,
    rows_out,
    rows_in,
    hidden_ref,
    part_out,
    part_x,
    part_sum,
    part_in,
    proj_out,
    proj_core,
    mid_out,
    proj_mid,
    last_out,
    proj_in,
    cot,
    cot_swap,
    state_t,
    grad_out,
    grad_in,
    load_sem,
    send_sem,
    recv_sem,
):
    token_rows, width = tokens_ref.shape
    rows = rows_out.shape[1]
    capacity, halves, rows_again = sizes(dp_count, expert_count, token_rows, top_count, width)
    assert rows == rows_again
    units = gate.shape[1]
    model_width = width * expert_count
    groups = expert_count // 4
    recv_at, _ = sem_plan(dp_count, groups)
    send_at = {name: i for i, name in enumerate(recv_at)}
    me_dp, me = lax.axis_index("dp"), lax.axis_index("expert")
    me_group, me_mid, me_low = lax.div(me, 4), lax.rem(lax.div(me, 2), 2), lax.rem(me, 2)
    own_first = me_dp * expert_count

    loads = [
        pltpu.make_async_copy(src, dst, load_sem.at[i])
        for i, (src, dst) in enumerate(
            [
                (tokens_hbm, tokens_ref),
                (routes_hbm, routes_ref),
                (prob_hbm, prob_ref),
                (mask_hbm, mask_ref),
                (gain_hbm, gain_ref),
                (target_hbm, target_ref),
                (kvw_hbm, kvw),
                (gate_hbm, gate),
                (up_hbm, up),
                (down_hbm, down),
            ]
        )
    ]
    for load in loads:
        load.start()

    def expert_at(group, mid, low):
        return group * 4 + mid * 2 + low

    barrier = pltpu.get_barrier_semaphore()
    for step in range(1, expert_count):
        pl.semaphore_signal(
            barrier,
            inc=1,
            device_id=(me_dp, lax.rem(me + step, expert_count)),
            device_id_type=pl.DeviceIdType.MESH,
        )
    for step in range(1, dp_count):
        pl.semaphore_signal(
            barrier,
            inc=1,
            device_id=(lax.rem(me_dp + step, dp_count), me),
            device_id_type=pl.DeviceIdType.MESH,
        )

    def send(name, number, src, dst, target):
        pltpu.make_async_remote_copy(
            src_ref=src,
            dst_ref=dst,
            send_sem=send_sem.at[send_at[name]],
            recv_sem=recv_sem.at[recv_at[name] + number],
            device_id=target,
            device_id_type=pl.DeviceIdType.MESH,
        ).start()

    def arrived(name, number, like):
        pltpu.make_async_copy(like, like, recv_sem.at[recv_at[name] + number]).wait()

    leaving = []

    def leaves(name, like):
        leaving.append((name, like))

    def to_group(name, step, source, landing, numbered):
        group = swapped(me_group, step)
        for turn in range(1 if step == 0 else 0, 4):
            other = group * 4 + lax.rem(lax.rem(me, 4) + turn, 4)
            send(name, step if numbered else 0, source.at[other], landing, (me_dp, other))

    def dispatch(name, source, landing, work):
        name_x = name + "_x"
        for step in reversed(range(groups)):
            to_group(name, step, source, landing.at[own_first + me], True)
        landing[own_first + me] = source[me]

        def forward(step):
            count = 3 if step == 0 else 4
            arrived(name, step, landing.at[pl.ds(0, count)])
            span = pl.ds(own_first + swapped(me_group, step) * 4, 4)
            for turn in range(1, dp_count):
                send(name_x, me_dp * groups + step, landing.at[span], landing.at[span], (lax.rem(me_dp + turn, dp_count), me))

        forward(0)
        for step in range(groups):
            if step + 1 < groups:
                forward(step + 1)
            for turn in range(1, dp_count):
                other = lax.rem(me_dp + turn, dp_count)
                arrived(name_x, other * groups + step, landing.at[pl.ds(0, 4)])
            work(swapped(me_group, step))
        leaves(name, landing.at[pl.ds(0, expert_count - 1)])
        leaves(name_x, landing.at[pl.ds(0, (dp_count - 1) * expert_count)])

    place_count = expert_count * rows
    older = lax.broadcasted_iota(jnp.int32, (token_rows, token_rows), 0)
    newer = lax.broadcasted_iota(jnp.int32, (token_rows, token_rows), 1)
    before = (older < newer).astype(f32).astype(bf16)
    same = older == newer

    loads[0].wait()
    loads[1].wait()
    names = lax.broadcasted_iota(jnp.int32, (expert_count, token_rows), 0)
    picks = [(names == routes_ref[k : k + 1, :]).astype(f32) for k in range(top_count)]
    counts = dot(sum(picks).astype(bf16), before, (1, 0))
    number = lax.broadcasted_iota(jnp.int32, (place_count, token_rows), 0)
    position = []
    for k in range(top_count):
        slot = jnp.sum(picks[k] * counts, axis=0, keepdims=True).astype(jnp.int32)
        position.append(routes_ref[k : k + 1, :] * rows + slot)
    sent_rows = jnp.zeros((place_count, 128), f32)
    for h in range(halves):
        both = jnp.zeros((place_count, token_rows), f32)
        for k in range(top_count):
            chosen = (number == position[k] + h * capacity).astype(f32)
            place[k, h] = chosen.astype(bf16)
            both = both + chosen
        sent_rows = sent_rows + dot(both.astype(bf16), tokens_ref[:, h * 128 : (h + 1) * 128], (1, 0))
    rows_out[...] = sent_rows.astype(bf16).reshape(expert_count, rows, 128)
    pl.semaphore_wait(barrier, expert_count - 1 + dp_count - 1)

    def column(row):
        return jnp.sum(jnp.where(same, row, 0), axis=1, keepdims=True)

    all_rows = dp_count * rows
    squares = [jnp.zeros((all_rows, 1), f32)]
    sums = [[jnp.zeros((all_rows, units), f32) for h in range(halves)] for _ in range(2)]

    for load in loads[2:6]:
        load.wait()

    def up_projections(group):
        if not squares[1:]:
            for load in loads[7:]:
                load.wait()
            squares.append(None)
        for i in range(4):
            f = group * 4 + i
            piece = jnp.concatenate([rows_in[b * expert_count + f] for b in range(dp_count)], axis=0).astype(f32)
            squares[0] = squares[0] + jnp.sum(piece * piece, axis=1, keepdims=True)
            for h in range(halves):
                span = pl.ds(pl.multiple_of(f * width + h * 128, 128), 128)
                gained = (piece * gain_ref[:, span]).astype(bf16)
                sums[0][h] = sums[0][h] + dot(gained, gate[span, :], (1, 0))
                sums[1][h] = sums[1][h] + dot(gained, up[span, :], (1, 0))

    dispatch("rows", rows_out, rows_in, up_projections)

    row_number = lax.broadcasted_iota(jnp.int32, (rows, 1), 0)
    for b in range(dp_count):
        span = slice(b * rows, (b + 1) * rows)

        def folded(terms):
            full = jnp.zeros(terms[0].shape, f32)
            for h, term in enumerate(terms):
                full = full + (pltpu.roll(term, rows - h * capacity, 0) if h else term)
            return jnp.where(row_number < capacity, full, 0.0)

        mean = folded([jnp.broadcast_to(squares[0][span], (rows, units))] * halves) / model_width
        scale = lax.rsqrt(mean + eps_norm)
        gate_val = folded([term[span] for term in sums[0]]) * scale
        up_val = folded([term[span] for term in sums[1]]) * scale
        hidden = gate_val / (1.0 + jnp.exp(-gate_val)) * up_val
        for h in range(halves):
            spread = pltpu.roll(hidden, h * capacity, 0) if h else hidden
            hidden_ref[h, span, :] = spread.astype(bf16)

    for step in reversed(range(groups)):
        group = swapped(me_group, step)
        for i in range(4):
            f = group * 4 + i
            piece = jnp.zeros((all_rows, 128), f32)
            for h in range(halves):
                span = pl.ds(pl.multiple_of(f * width + h * 128, 128), 128)
                piece = piece + dot(hidden_ref[h], down[:, span], (1, 0))
            piece = piece.astype(bf16)
            for b in range(dp_count):
                part_out[b * expert_count + f] = piece[b * rows : (b + 1) * rows]
        for turn in range(1, dp_count):
            other = lax.rem(me_dp + turn, dp_count)
            send(
                "part_x",
                me_dp * groups + step,
                part_out.at[pl.ds(other * expert_count + group * 4, 4)],
                part_x.at[pl.ds(own_first + group * 4, 4)],
                (other, me),
            )

    def column_work():
        gather = []
        for k in range(top_count):
            spot = column(position[k])
            lanes = lax.broadcasted_iota(jnp.int32, (token_rows, place_count), 1)
            gather.append([(lanes == spot + h * capacity).astype(f32).astype(bf16) for h in range(halves)])
        return gather, [column(prob_ref[k : k + 1, :]) for k in range(top_count)]

    gather, prob_column = column_work()
    loads[6].wait()
    own_keys = kvw.shape[1] // expert_count
    turned = kvw[...].T
    for g in range(groups):
        for mid in range(2):
            for low in range(2):
                c = expert_at(g, mid, low)
                kvw_t[low, mid, g] = turned[c * own_keys : (c + 1) * own_keys]
    target = target_ref[...].astype(f32).T

    for step in reversed(range(groups)):
        group = swapped(me_group, step)
        total = part_out[pl.ds(own_first + group * 4, 4)].astype(f32)
        for turn in range(1, dp_count):
            other = lax.rem(me_dp + turn, dp_count)
            arrived("part_x", other * groups + step, part_x.at[pl.ds(0, 4)])
            total = total + part_x[pl.ds(other * expert_count + group * 4, 4)].astype(f32)
        part_sum[pl.ds(group * 4, 4)] = total.astype(bf16)
        to_group("part", step, part_sum, part_in.at[me], False)
    leaves("part_x", part_out.at[pl.ds(0, (dp_count - 1) * expert_count)])
    leaves("part", part_in.at[pl.ds(0, expert_count - 1)])
    part_in[me] = part_sum[me]
    arrived("part", 0, part_in.at[pl.ds(0, expert_count - 1)])

    expert_out = part_in[...].reshape(place_count, 128)
    states = []
    for h in range(halves):
        state = tokens_ref[:, h * 128 : (h + 1) * 128].astype(f32)
        for k in range(top_count):
            state = state + prob_column[k] * dot(gather[k][h], expert_out, (1, 0))
        states.append(state)
    state_wide = jnp.concatenate(states, axis=1) if halves > 1 else states[0]
    state = state_wide.astype(bf16)

    def project(low, mid):
        weights = kvw_t[low, mid].reshape(groups * own_keys, width)
        return dot(weights, state, (1, 1)).reshape(groups, own_keys, token_rows)

    sibling = (me_dp, expert_at(me_group, me_mid, 1 - me_low))
    across = (me_dp, expert_at(me_group, 1 - me_mid, me_low))
    for turn, mid in enumerate((1 - me_mid, me_mid)):
        proj_out[turn] = project(1 - me_low, mid).astype(bf16)
        send("proj_core", turn, proj_out.at[turn], proj_core.at[turn], sibling)
    leaves("proj_core", proj_out)
    far, near = project(me_low, 1 - me_mid), project(me_low, me_mid)
    arrived("proj_core", 0, proj_core.at[0])
    mid_out[...] = (far + proj_core[0].astype(f32)).astype(bf16)
    for step in reversed(range(groups)):
        group = swapped(me_group, step)
        send("proj_mid", step, mid_out.at[group], proj_mid.at[group], across)
    leaves("proj_mid", proj_mid)
    arrived("proj_core", 1, proj_core.at[1])
    proj_core[1] = (near + proj_core[1].astype(f32)).astype(bf16)
    state_t[me_dp] = state_wide.T.astype(bf16)
    for turn in range(1, dp_count):
        send("state", 0, state_t.at[me_dp], state_t.at[me_dp], (lax.rem(me_dp + turn, dp_count), me))
    leaves("state", state_t.at[pl.ds(0, dp_count - 1)])
    key_value = None
    for step in reversed(range(groups)):
        group = swapped(me_group, step)
        arrived("proj_mid", step, proj_mid.at[0])
        summed = proj_core[1, group].astype(f32) + proj_mid[group].astype(f32)
        if step:
            last_out[group] = summed.astype(bf16)
            send("proj", 0, last_out.at[group], proj_in.at[me_group], (me_dp, expert_at(group, me_mid, me_low)))
        else:
            proj_in[me_group] = jnp.zeros(proj_in.shape[1:], bf16)
            key_value = summed
    leaves("proj", proj_in.at[pl.ds(0, groups - 1)])
    arrived("proj", 0, proj_in.at[pl.ds(0, groups - 1)])
    key_value = key_value + jnp.sum(proj_in[...].astype(f32), axis=0)
    cot[me] = (mask_ref[...].astype(f32) * (key_value - target) * token_rows ** (-0.5)).astype(bf16)

    for step in reversed(range(1, groups)):
        other = expert_at(swapped(me_group, step), me_mid, me_low)
        send("cot", step, cot.at[me], cot.at[me], (me_dp, other))
    for step in range(groups):
        if step:
            arrived("cot", step, cot.at[0])
        c = expert_at(swapped(me_group, step), me_mid, me_low)
        send("cot_mid", step, cot.at[c], cot.at[c], across)
        send("cot_core", 0, cot.at[c], cot.at[c], sibling)
    for step in range(groups):
        arrived("cot_mid", step, cot.at[0])
        c = expert_at(swapped(me_group, step), 1 - me_mid, me_low)
        send("cot_core", 0, cot.at[c], cot.at[c], sibling)
    leaves("cot", cot.at[pl.ds(0, groups - 1)])
    leaves("cot_mid", cot.at[pl.ds(0, groups)])
    leaves("cot_core", cot.at[pl.ds(0, 2 * groups)])

    share = expert_count // dp_count
    pairs = share // 2
    swap_bytes = cot_swap.at[pl.ds(0, (dp_count - 1) * pairs)]
    for turn in range(1, dp_count):
        other = lax.rem(me_dp + turn, dp_count)
        for i in range(pairs):
            part = 2 * i + me_low
            send("swap", 0, cot.at[other * share + part], cot_swap.at[me_dp * share + part], (other, me))
    leaves("swap", swap_bytes)
    arrived("cot_core", 0, cot.at[pl.ds(0, 2 * groups)])

    state_grad_t = dot(kvw[...], cot[...].reshape(kvw.shape[1], token_rows), (1, 0))
    grads = jnp.zeros((place_count, 128), f32)
    for k in range(top_count):
        pair_grad = (state_grad_t * prob_ref[k : k + 1, :]).astype(bf16)
        for h in range(halves):
            grads = grads + dot(place[k, h], pair_grad[h * 128 : (h + 1) * 128], (1, 1))
    grad_out[...] = grads.astype(bf16).reshape(expert_count, rows, 128)

    hidden_t = [hidden_ref[h].astype(f32).T.astype(bf16) for h in range(halves)]

    def down_gradient(group):
        for i in range(4):
            f = group * 4 + i
            piece = jnp.concatenate([grad_in[b * expert_count + f] for b in range(dp_count)], axis=0)
            for h in range(halves):
                span = pl.ds(pl.multiple_of(f * width + h * 128, 128), 128)
                down_grad_ref[:, span] = dot(hidden_t[h], piece, (1, 0)).astype(bf16)

    dispatch("grad", grad_out, grad_in, down_gradient)

    arrived("swap", 0, swap_bytes)
    for turn in range(1, dp_count):
        other = lax.rem(me_dp + turn, dp_count)
        for i in range(pairs):
            spot = cot_swap.at[other * share + 2 * i + me_low]
            send("swap_core", 0, spot, spot, sibling)
    leaves("swap_core", swap_bytes)
    columns = kv_grad_ref.shape[1]
    kv_grad = dot(state_t[me_dp], cot[pl.ds(me_dp * share, share)].reshape(columns, token_rows), (1, 1))
    arrived("state", 0, state_t.at[pl.ds(0, dp_count - 1)])
    arrived("swap_core", 0, swap_bytes)
    for turn in range(1, dp_count):
        other = lax.rem(me_dp + turn, dp_count)
        theirs = cot_swap[pl.ds(other * share, share)].reshape(columns, token_rows)
        kv_grad = kv_grad + dot(state_t[other], theirs, (1, 1))
    kv_grad_ref[...] = kv_grad

    for name, like in leaving:
        pltpu.make_async_copy(like, like, send_sem.at[send_at[name]]).wait()


def per_device(
    tokens,
    norm_gain,
    routes,
    route_prob,
    gate_weight,
    up_weight,
    down_weight,
    key_value_weight,
    key_value_target,
    concept_mask,
):
    token_rows, width = tokens.shape
    top_count = routes.shape[1]
    dp_count, expert_count = lax.axis_size("dp"), lax.axis_size("expert")
    device_count = dp_count * expert_count
    capacity, halves, rows = sizes(dp_count, expert_count, token_rows, top_count, width)
    groups = expert_count // 4
    model_width, units = gate_weight.shape[1:]
    keys = key_value_weight.shape[1]
    own_keys = keys // expert_count
    in_vmem = pl.BlockSpec(memory_space=pltpu.VMEM)
    in_any = pl.BlockSpec(memory_space=pl.ANY)
    pieces = pltpu.VMEM((device_count, rows, 128), bf16)
    own_pieces = pltpu.VMEM((expert_count, rows, 128), bf16)
    group_keys = pltpu.VMEM((groups, own_keys, token_rows), bf16)
    core_keys = pltpu.VMEM((2, groups, own_keys, token_rows), bf16)
    all_keys = pltpu.VMEM((expert_count, own_keys, token_rows), bf16)
    plan, recv_count = sem_plan(dp_count, groups)
    given = (
        tokens,
        routes.T,
        route_prob.T,
        concept_mask[None, :],
        norm_gain[None, :],
        key_value_target,
        key_value_weight,
        gate_weight[0],
        up_weight[0],
        down_weight[0],
    )
    down_grad, kv_grad = pl.pallas_call(
        functools.partial(kernel, dp_count, expert_count, top_count),
        out_shape=(
            jax.ShapeDtypeStruct((units, model_width), bf16),
            jax.ShapeDtypeStruct((width, keys // dp_count), f32),
        ),
        in_specs=[in_any] * len(given),
        out_specs=(in_vmem, in_vmem),
        scratch_shapes=[pltpu.VMEM(x.shape, x.dtype) for x in given]
        + [
            pltpu.VMEM((2, 2, groups, own_keys, width), bf16),
            pltpu.VMEM((top_count, halves, expert_count * rows, token_rows), bf16),
            own_pieces,
            pieces,
            pltpu.VMEM((halves, dp_count * rows, units), bf16),
            pieces,
            pieces,
            own_pieces,
            own_pieces,
            core_keys,
            core_keys,
            group_keys,
            group_keys,
            group_keys,
            group_keys,
            all_keys,
            all_keys,
            pltpu.VMEM((dp_count, width, token_rows), bf16),
            own_pieces,
            pieces,
            pltpu.SemaphoreType.DMA((len(given),)),
            pltpu.SemaphoreType.DMA((len(plan),)),
            pltpu.SemaphoreType.DMA((recv_count,)),
        ],
        compiler_params=pltpu.CompilerParams(
            collective_id=0, has_side_effects=True, vmem_limit_bytes=62 * 1024 * 1024
        ),
    )(*given)
    return (down_grad[None], kv_grad)


def solution(mesh):
    placed = (
        P("dp", "expert"),
        P(),
        P("dp", None),
        P("dp", None),
        P("expert", None, "dp"),
        P("expert", None, "dp"),
        P("expert", "dp", None),
        P("expert", None),
        P("dp", "expert"),
        P("dp"),
    )
    return jax.shard_map(
        per_device,
        mesh=mesh,
        in_specs=placed,
        out_specs=(P("expert", "dp", None), P("expert", "dp")),
        check_vma=False,
    )
```

```python
import functools

import jax
import jax.numpy as jnp
from jax import lax
from jax.experimental import pallas as pl
from jax.experimental.pallas import tpu as pltpu
from jax.sharding import PartitionSpec as P

eps_norm = 1e-06
f32, bf16 = jnp.float32, jnp.bfloat16


def dot(a, b, contract):
    return lax.dot_general(a, b, ((contract[:1], contract[1:]), ((), ())), preferred_element_type=f32)


def swapped(index, step):
    bit = 1
    while bit <= step:
        if step & bit:
            index = index + bit - 2 * bit * lax.rem(lax.div(index, bit), 2)
        bit *= 2
    return index


def sizes(dp_count, expert_count, token_rows, top_count, width):
    capacity = 5 * token_rows * top_count // (4 * expert_count)
    halves = width // 128
    return capacity, halves, -(-halves * capacity // 16) * 16


def sem_plan(dp_count, groups):
    plan, at = {}, 0
    for name, count in (
        ("rows", groups),
        ("rows_x", dp_count * groups),
        ("part_x", dp_count * groups),
        ("part", 1),
        ("proj_core", 2),
        ("proj_mid", groups),
        ("proj", 1),
        ("state", 1),
        ("cot", groups),
        ("cot_mid", groups),
        ("cot_core", 1),
        ("swap", 1),
        ("swap_core", 1),
        ("grad", groups),
        ("grad_x", dp_count * groups),
    ):
        plan[name] = at
        at += count
    return plan, at


def kernel(
    dp_count,
    expert_count,
    top_count,
    tokens_hbm,
    routes_hbm,
    prob_hbm,
    mask_hbm,
    gain_hbm,
    target_hbm,
    kvw_hbm,
    gate_hbm,
    up_hbm,
    down_hbm,
    down_grad_ref,
    kv_grad_ref,
    tokens_ref,
    routes_ref,
    prob_ref,
    mask_ref,
    gain_ref,
    target_ref,
    kvw,
    gate,
    up,
    down,
    kvw_t,
    place,
    rows_out,
    rows_in,
    hidden_ref,
    part_out,
    part_x,
    part_sum,
    part_in,
    proj_out,
    proj_core,
    mid_out,
    proj_mid,
    last_out,
    proj_in,
    cot,
    cot_swap,
    state_t,
    grad_out,
    grad_in,
    load_sem,
    send_sem,
    recv_sem,
):
    token_rows, width = tokens_ref.shape
    rows = rows_out.shape[1]
    capacity, halves, rows_again = sizes(dp_count, expert_count, token_rows, top_count, width)
    assert rows == rows_again
    units = gate.shape[1]
    model_width = width * expert_count
    groups = expert_count // 4
    recv_at, _ = sem_plan(dp_count, groups)
    send_at = {name: i for i, name in enumerate(recv_at)}
    me_dp, me = lax.axis_index("dp"), lax.axis_index("expert")
    me_group, me_mid, me_low = lax.div(me, 4), lax.rem(lax.div(me, 2), 2), lax.rem(me, 2)
    own_first = me_dp * expert_count

    loads = [
        pltpu.make_async_copy(src, dst, load_sem.at[i])
        for i, (src, dst) in enumerate(
            [
                (tokens_hbm, tokens_ref),
                (routes_hbm, routes_ref),
                (prob_hbm, prob_ref),
                (mask_hbm, mask_ref),
                (gain_hbm, gain_ref),
                (target_hbm, target_ref),
                (kvw_hbm, kvw),
                (gate_hbm, gate),
                (up_hbm, up),
                (down_hbm, down),
            ]
        )
    ]
    for load in loads:
        load.start()

    def expert_at(group, mid, low):
        return group * 4 + mid * 2 + low

    barrier = pltpu.get_barrier_semaphore()
    for step in range(1, expert_count):
        pl.semaphore_signal(
            barrier,
            inc=1,
            device_id=(me_dp, lax.rem(me + step, expert_count)),
            device_id_type=pl.DeviceIdType.MESH,
        )
    for step in range(1, dp_count):
        pl.semaphore_signal(
            barrier,
            inc=1,
            device_id=(lax.rem(me_dp + step, dp_count), me),
            device_id_type=pl.DeviceIdType.MESH,
        )

    def send(name, number, src, dst, target):
        pltpu.make_async_remote_copy(
            src_ref=src,
            dst_ref=dst,
            send_sem=send_sem.at[send_at[name]],
            recv_sem=recv_sem.at[recv_at[name] + number],
            device_id=target,
            device_id_type=pl.DeviceIdType.MESH,
        ).start()

    def arrived(name, number, like):
        pltpu.make_async_copy(like, like, recv_sem.at[recv_at[name] + number]).wait()

    leaving = []

    def leaves(name, like):
        leaving.append((name, like))

    def to_group(name, step, source, landing, numbered):
        group = swapped(me_group, step)
        for turn in range(1 if step == 0 else 0, 4):
            other = group * 4 + lax.rem(lax.rem(me, 4) + turn, 4)
            send(name, step if numbered else 0, source.at[other], landing, (me_dp, other))

    def dispatch(name, source, landing, work, beside):
        name_x = name + "_x"
        for step in reversed(range(groups)):
            to_group(name, step, source, landing.at[own_first + me], True)
        landing[own_first + me] = source[me]

        def forward(step):
            count = 3 if step == 0 else 4
            arrived(name, step, landing.at[pl.ds(0, count)])
            span = pl.ds(own_first + swapped(me_group, step) * 4, 4)
            for turn in range(1, dp_count):
                send(name_x, me_dp * groups + step, landing.at[span], landing.at[span], (lax.rem(me_dp + turn, dp_count), me))

        forward(0)
        beside(0)
        for step in range(groups):
            if step + 1 < groups:
                forward(step + 1)
                beside(step + 1)
            for turn in range(1, dp_count):
                other = lax.rem(me_dp + turn, dp_count)
                arrived(name_x, other * groups + step, landing.at[pl.ds(0, 4)])
            work(swapped(me_group, step))
        leaves(name, landing.at[pl.ds(0, expert_count - 1)])
        leaves(name_x, landing.at[pl.ds(0, (dp_count - 1) * expert_count)])

    place_count = expert_count * rows
    older = lax.broadcasted_iota(jnp.int32, (token_rows, token_rows), 0)
    newer = lax.broadcasted_iota(jnp.int32, (token_rows, token_rows), 1)
    before = (older < newer).astype(f32).astype(bf16)
    same = older == newer

    loads[0].wait()
    loads[1].wait()
    names = lax.broadcasted_iota(jnp.int32, (expert_count, token_rows), 0)
    picks = [(names == routes_ref[k : k + 1, :]).astype(f32) for k in range(top_count)]
    counts = dot(sum(picks).astype(bf16), before, (1, 0))
    number = lax.broadcasted_iota(jnp.int32, (place_count, token_rows), 0)
    position = []
    for k in range(top_count):
        slot = jnp.sum(picks[k] * counts, axis=0, keepdims=True).astype(jnp.int32)
        position.append(routes_ref[k : k + 1, :] * rows + slot)
    placed, parts = [], []
    for h in range(halves):
        both = jnp.zeros((place_count, token_rows), f32)
        for k in range(top_count):
            at = (h * top_count + k) * token_rows
            chosen = (number == position[k] + h * capacity).astype(f32)
            place[:, at : at + token_rows] = chosen.astype(bf16)
            both = both + chosen
        placed.append(both.astype(bf16))
        parts.append(tokens_ref[:, h * 128 : (h + 1) * 128])
    sent_rows = dot(jnp.concatenate(placed, axis=1), jnp.concatenate(parts, axis=0), (1, 0))
    rows_out[...] = sent_rows.astype(bf16).reshape(expert_count, rows, 128)
    pl.semaphore_wait(barrier, expert_count - 1 + dp_count - 1)

    def column(row):
        return jnp.sum(jnp.where(same, row, 0), axis=1, keepdims=True)

    all_rows = dp_count * rows
    squares = [jnp.zeros((all_rows, 1), f32)]
    sums = [jnp.zeros((all_rows, 2 * units), f32)]
    block_row = lax.rem(lax.broadcasted_iota(jnp.int32, (all_rows, 1), 0), rows)
    in_half = [(block_row >= h * capacity) & (block_row < (h + 1) * capacity) for h in range(halves)]

    for load in loads[2:6]:
        load.wait()

    def up_projections(group):
        if not squares[1:]:
            for load in loads[7:]:
                load.wait()
            squares.append(None)
        sides, weights = [], []
        for i in range(4):
            f = group * 4 + i
            piece = jnp.concatenate([rows_in[b * expert_count + f] for b in range(dp_count)], axis=0).astype(f32)
            squares[0] = squares[0] + jnp.sum(piece * piece, axis=1, keepdims=True)
            for h in range(halves):
                span = pl.ds(pl.multiple_of(f * width + h * 128, 128), 128)
                sides.append(jnp.where(in_half[h], piece * gain_ref[:, span], 0.0).astype(bf16))
            span = pl.ds(pl.multiple_of(f * width, 128), width)
            weights.append(jnp.concatenate([gate[span, :], up[span, :]], axis=1))
        sums[0] = sums[0] + dot(jnp.concatenate(sides, axis=1), jnp.concatenate(weights, axis=0), (1, 0))

    dispatch("rows", rows_out, rows_in, up_projections, lambda step: None)

    row_number = lax.broadcasted_iota(jnp.int32, (rows, 1), 0)
    for b in range(dp_count):
        span = slice(b * rows, (b + 1) * rows)

        def folded(term):
            full = term
            for h in range(1, halves):
                full = full + pltpu.roll(term, rows - h * capacity, 0)
            return jnp.where(row_number < capacity, full, 0.0)

        mean = folded(jnp.broadcast_to(squares[0][span], (rows, units))) / model_width
        scale = lax.rsqrt(mean + eps_norm)
        gate_val = folded(sums[0][span, :units]) * scale
        up_val = folded(sums[0][span, units:]) * scale
        hidden = gate_val / (1.0 + jnp.exp(-gate_val)) * up_val
        for h in range(halves):
            spread = pltpu.roll(hidden, h * capacity, 0) if h else hidden
            hidden_ref[span, h * units : (h + 1) * units] = spread.astype(bf16)

    for step in reversed(range(groups)):
        group = swapped(me_group, step)
        for i in range(4):
            f = group * 4 + i
            spans = [pl.ds(pl.multiple_of(f * width + h * 128, 128), 128) for h in range(halves)]
            weights = jnp.concatenate([down[:, span] for span in spans], axis=0)
            piece = dot(hidden_ref[...], weights, (1, 0)).astype(bf16)
            for b in range(dp_count):
                part_out[b * expert_count + f] = piece[b * rows : (b + 1) * rows]
        for turn in range(1, dp_count):
            other = lax.rem(me_dp + turn, dp_count)
            send(
                "part_x",
                me_dp * groups + step,
                part_out.at[pl.ds(other * expert_count + group * 4, 4)],
                part_x.at[pl.ds(own_first + group * 4, 4)],
                (other, me),
            )

    def column_work():
        gather = []
        for k in range(top_count):
            spot = column(position[k])
            lanes = lax.broadcasted_iota(jnp.int32, (token_rows, place_count), 1)
            gather.append([(lanes == spot + h * capacity).astype(f32).astype(bf16) for h in range(halves)])
        return gather, [column(prob_ref[k : k + 1, :]) for k in range(top_count)]

    gather, prob_column = column_work()
    hidden_t = hidden_ref[...].astype(f32).T.astype(bf16)
    loads[6].wait()
    own_keys = kvw.shape[1] // expert_count
    turned = kvw[...].T
    for g in range(groups):
        for mid in range(2):
            for low in range(2):
                c = expert_at(g, mid, low)
                kvw_t[low, mid, g] = turned[c * own_keys : (c + 1) * own_keys]
    target = target_ref[...].astype(f32).T

    for step in reversed(range(groups)):
        group = swapped(me_group, step)
        total = part_out[pl.ds(own_first + group * 4, 4)].astype(f32)
        for turn in range(1, dp_count):
            other = lax.rem(me_dp + turn, dp_count)
            arrived("part_x", other * groups + step, part_x.at[pl.ds(0, 4)])
            total = total + part_x[pl.ds(other * expert_count + group * 4, 4)].astype(f32)
        part_sum[pl.ds(group * 4, 4)] = total.astype(bf16)
        to_group("part", step, part_sum, part_in.at[me], False)
    leaves("part_x", part_out.at[pl.ds(0, (dp_count - 1) * expert_count)])
    leaves("part", part_in.at[pl.ds(0, expert_count - 1)])
    part_in[me] = part_sum[me]
    arrived("part", 0, part_in.at[pl.ds(0, expert_count - 1)])

    expert_out = part_in[...].reshape(place_count, 128)
    states = []
    for h in range(halves):
        state = tokens_ref[:, h * 128 : (h + 1) * 128].astype(f32)
        for k in range(top_count):
            state = state + prob_column[k] * dot(gather[k][h], expert_out, (1, 0))
        states.append(state)
    state_wide = jnp.concatenate(states, axis=1) if halves > 1 else states[0]
    state = state_wide.astype(bf16)

    def project(low, mid):
        weights = kvw_t[low, mid].reshape(groups * own_keys, width)
        return dot(weights, state, (1, 1)).reshape(groups, own_keys, token_rows)

    sibling = (me_dp, expert_at(me_group, me_mid, 1 - me_low))
    across = (me_dp, expert_at(me_group, 1 - me_mid, me_low))
    for turn, mid in enumerate((1 - me_mid, me_mid)):
        proj_out[turn] = project(1 - me_low, mid).astype(bf16)
        send("proj_core", turn, proj_out.at[turn], proj_core.at[turn], sibling)
    leaves("proj_core", proj_out)
    far, near = project(me_low, 1 - me_mid), project(me_low, me_mid)
    arrived("proj_core", 0, proj_core.at[0])
    mid_out[...] = (far + proj_core[0].astype(f32)).astype(bf16)
    for step in reversed(range(groups)):
        group = swapped(me_group, step)
        send("proj_mid", step, mid_out.at[group], proj_mid.at[group], across)
    leaves("proj_mid", proj_mid)
    arrived("proj_core", 1, proj_core.at[1])
    proj_core[1] = (near + proj_core[1].astype(f32)).astype(bf16)
    state_t[me_dp] = state_wide.T.astype(bf16)
    for turn in range(1, dp_count):
        send("state", 0, state_t.at[me_dp], state_t.at[me_dp], (lax.rem(me_dp + turn, dp_count), me))
    leaves("state", state_t.at[pl.ds(0, dp_count - 1)])
    key_value = None
    for step in reversed(range(groups)):
        group = swapped(me_group, step)
        arrived("proj_mid", step, proj_mid.at[0])
        summed = proj_core[1, group].astype(f32) + proj_mid[group].astype(f32)
        if step:
            last_out[group] = summed.astype(bf16)
            send("proj", 0, last_out.at[group], proj_in.at[me_group], (me_dp, expert_at(group, me_mid, me_low)))
        else:
            proj_in[me_group] = jnp.zeros(proj_in.shape[1:], bf16)
            key_value = summed
    leaves("proj", proj_in.at[pl.ds(0, groups - 1)])
    arrived("proj", 0, proj_in.at[pl.ds(0, groups - 1)])
    key_value = key_value + jnp.sum(proj_in[...].astype(f32), axis=0)
    cot[me] = (mask_ref[...].astype(f32) * (key_value - target) * token_rows ** (-0.5)).astype(bf16)

    for step in reversed(range(1, groups)):
        other = expert_at(swapped(me_group, step), me_mid, me_low)
        send("cot", step, cot.at[me], cot.at[me], (me_dp, other))
    for step in range(groups):
        if step:
            arrived("cot", step, cot.at[0])
        c = expert_at(swapped(me_group, step), me_mid, me_low)
        send("cot_mid", step, cot.at[c], cot.at[c], across)
        send("cot_core", 0, cot.at[c], cot.at[c], sibling)
    for step in range(groups):
        arrived("cot_mid", step, cot.at[0])
        c = expert_at(swapped(me_group, step), 1 - me_mid, me_low)
        send("cot_core", 0, cot.at[c], cot.at[c], sibling)
    leaves("cot", cot.at[pl.ds(0, groups - 1)])
    leaves("cot_mid", cot.at[pl.ds(0, groups)])
    leaves("cot_core", cot.at[pl.ds(0, 2 * groups)])

    share = expert_count // dp_count
    pairs = share // 2
    swap_bytes = cot_swap.at[pl.ds(0, (dp_count - 1) * pairs)]
    for turn in range(1, dp_count):
        other = lax.rem(me_dp + turn, dp_count)
        for i in range(pairs):
            part = 2 * i + me_low
            send("swap", 0, cot.at[other * share + part], cot_swap.at[me_dp * share + part], (other, me))
    leaves("swap", swap_bytes)
    arrived("cot_core", 0, cot.at[pl.ds(0, 2 * groups)])

    state_grad_t = dot(kvw[...], cot[...].reshape(kvw.shape[1], token_rows), (1, 0))
    pair_grads = [(state_grad_t * prob_ref[k : k + 1, :]).astype(bf16) for k in range(top_count)]
    sides = [pair_grads[k][h * 128 : (h + 1) * 128] for h in range(halves) for k in range(top_count)]
    grads = dot(place[...], jnp.concatenate(sides, axis=1), (1, 1))
    grad_out[...] = grads.astype(bf16).reshape(expert_count, rows, 128)

    columns = kv_grad_ref.shape[1]

    def beside_grads(step):
        if step == 0:
            own = cot[pl.ds(me_dp * share, share)].reshape(columns, token_rows)
            kv_grad_ref[...] = dot(state_t[me_dp], own, (1, 1))
        if step == 1:
            arrived("swap", 0, swap_bytes)
            for turn in range(1, dp_count):
                other = lax.rem(me_dp + turn, dp_count)
                for i in range(pairs):
                    spot = cot_swap.at[other * share + 2 * i + me_low]
                    send("swap_core", 0, spot, spot, sibling)
            leaves("swap_core", swap_bytes)
        if step == groups - 1:
            arrived("state", 0, state_t.at[pl.ds(0, dp_count - 1)])
            arrived("swap_core", 0, swap_bytes)
            for turn in range(1, dp_count):
                other = lax.rem(me_dp + turn, dp_count)
                theirs = cot_swap[pl.ds(other * share, share)].reshape(columns, token_rows)
                kv_grad_ref[...] += dot(state_t[other], theirs, (1, 1))

    def down_gradient(group):
        pieces = []
        for i in range(4):
            f = group * 4 + i
            pieces.append(jnp.concatenate([grad_in[b * expert_count + f] for b in range(dp_count)], axis=0))
        wide = dot(hidden_t, jnp.concatenate(pieces, axis=1), (1, 0)).astype(bf16)
        for i in range(4):
            for h in range(halves):
                span = pl.ds(pl.multiple_of((group * 4 + i) * width + h * 128, 128), 128)
                down_grad_ref[:, span] = wide[h * units : (h + 1) * units, i * 128 : (i + 1) * 128]

    dispatch("grad", grad_out, grad_in, down_gradient, beside_grads)

    for name, like in leaving:
        pltpu.make_async_copy(like, like, send_sem.at[send_at[name]]).wait()


def per_device(
    tokens,
    norm_gain,
    routes,
    route_prob,
    gate_weight,
    up_weight,
    down_weight,
    key_value_weight,
    key_value_target,
    concept_mask,
):
    token_rows, width = tokens.shape
    top_count = routes.shape[1]
    dp_count, expert_count = lax.axis_size("dp"), lax.axis_size("expert")
    device_count = dp_count * expert_count
    capacity, halves, rows = sizes(dp_count, expert_count, token_rows, top_count, width)
    groups = expert_count // 4
    model_width, units = gate_weight.shape[1:]
    keys = key_value_weight.shape[1]
    own_keys = keys // expert_count
    in_vmem = pl.BlockSpec(memory_space=pltpu.VMEM)
    in_any = pl.BlockSpec(memory_space=pl.ANY)
    pieces = pltpu.VMEM((device_count, rows, 128), bf16)
    own_pieces = pltpu.VMEM((expert_count, rows, 128), bf16)
    group_keys = pltpu.VMEM((groups, own_keys, token_rows), bf16)
    core_keys = pltpu.VMEM((2, groups, own_keys, token_rows), bf16)
    all_keys = pltpu.VMEM((expert_count, own_keys, token_rows), bf16)
    plan, recv_count = sem_plan(dp_count, groups)
    given = (
        tokens,
        routes.T,
        route_prob.T,
        concept_mask[None, :],
        norm_gain[None, :],
        key_value_target,
        key_value_weight,
        gate_weight[0],
        up_weight[0],
        down_weight[0],
    )
    down_grad, kv_grad = pl.pallas_call(
        functools.partial(kernel, dp_count, expert_count, top_count),
        out_shape=(
            jax.ShapeDtypeStruct((units, model_width), bf16),
            jax.ShapeDtypeStruct((width, keys // dp_count), f32),
        ),
        in_specs=[in_any] * len(given),
        out_specs=(in_vmem, in_vmem),
        scratch_shapes=[pltpu.VMEM(x.shape, x.dtype) for x in given]
        + [
            pltpu.VMEM((2, 2, groups, own_keys, width), bf16),
            pltpu.VMEM((expert_count * rows, halves * top_count * token_rows), bf16),
            own_pieces,
            pieces,
            pltpu.VMEM((dp_count * rows, halves * units), bf16),
            pieces,
            pieces,
            own_pieces,
            own_pieces,
            core_keys,
            core_keys,
            group_keys,
            group_keys,
            group_keys,
            group_keys,
            all_keys,
            all_keys,
            pltpu.VMEM((dp_count, width, token_rows), bf16),
            own_pieces,
            pieces,
            pltpu.SemaphoreType.DMA((len(given),)),
            pltpu.SemaphoreType.DMA((len(plan),)),
            pltpu.SemaphoreType.DMA((recv_count,)),
        ],
        compiler_params=pltpu.CompilerParams(
            collective_id=0, has_side_effects=True, vmem_limit_bytes=61 * 1024 * 1024 + 256 * 1024
        ),
    )(*given)
    return (down_grad[None], kv_grad)


def solution(mesh):
    placed = (
        P("dp", "expert"),
        P(),
        P("dp", None),
        P("dp", None),
        P("expert", None, "dp"),
        P("expert", None, "dp"),
        P("expert", "dp", None),
        P("expert", None),
        P("dp", "expert"),
        P("dp"),
    )
    return jax.shard_map(
        per_device,
        mesh=mesh,
        in_specs=placed,
        out_specs=(P("expert", "dp", None), P("expert", "dp")),
        check_vma=False,
    )
```

```python
import functools

import jax
import jax.numpy as jnp
from jax import lax
from jax.experimental import pallas as pl
from jax.experimental.pallas import tpu as pltpu
from jax.sharding import PartitionSpec as P

eps_norm = 1e-06
f32, bf16 = jnp.float32, jnp.bfloat16


def dot(a, b, contract):
    return lax.dot_general(a, b, ((contract[:1], contract[1:]), ((), ())), preferred_element_type=f32)


def swapped(index, step):
    bit = 1
    while bit <= step:
        if step & bit:
            index = index + bit - 2 * bit * lax.rem(lax.div(index, bit), 2)
        bit *= 2
    return index


def sizes(dp_count, expert_count, token_rows, top_count, width):
    capacity = 5 * token_rows * top_count // (4 * expert_count)
    halves = width // 128
    return capacity, halves, -(-halves * capacity // 16) * 16


def sem_plan(dp_count, groups):
    plan, at = {}, 0
    for name, count in (
        ("rows", groups),
        ("rows_x", dp_count * groups),
        ("part_x", dp_count * groups),
        ("part", 1),
        ("proj_core", 2),
        ("proj_mid", groups),
        ("proj", 1),
        ("state", 1),
        ("cot", groups),
        ("cot_mid", groups),
        ("cot_core", 1),
        ("swap", 1),
        ("swap_core", 1),
        ("grad", groups),
        ("grad_x", dp_count * groups),
    ):
        plan[name] = at
        at += count
    return plan, at


def kernel(
    dp_count,
    expert_count,
    top_count,
    tokens_hbm,
    routes_hbm,
    prob_hbm,
    mask_hbm,
    gain_hbm,
    target_hbm,
    kvw_hbm,
    gate_hbm,
    up_hbm,
    down_hbm,
    down_grad_ref,
    kv_grad_ref,
    tokens_ref,
    routes_ref,
    prob_ref,
    mask_ref,
    gain_ref,
    target_ref,
    kvw,
    gate,
    up,
    down,
    kvw_t,
    place,
    rows_out,
    rows_in,
    hidden_ref,
    part_out,
    part_x,
    part_sum,
    part_in,
    proj_out,
    proj_core,
    mid_out,
    proj_mid,
    last_out,
    proj_in,
    cot,
    cot_swap,
    state_t,
    grad_out,
    grad_in,
    load_sem,
    send_sem,
    recv_sem,
):
    token_rows, width = tokens_ref.shape
    rows = rows_out.shape[1]
    capacity, halves, rows_again = sizes(dp_count, expert_count, token_rows, top_count, width)
    assert rows == rows_again
    units = gate.shape[1]
    model_width = width * expert_count
    groups = expert_count // 4
    recv_at, _ = sem_plan(dp_count, groups)
    send_at = {name: i for i, name in enumerate(recv_at)}
    me_dp, me = lax.axis_index("dp"), lax.axis_index("expert")
    me_group, me_mid, me_low = lax.div(me, 4), lax.rem(lax.div(me, 2), 2), lax.rem(me, 2)
    own_first = me_dp * expert_count

    loads = [
        pltpu.make_async_copy(src, dst, load_sem.at[i])
        for i, (src, dst) in enumerate(
            [
                (tokens_hbm, tokens_ref),
                (routes_hbm, routes_ref),
                (prob_hbm, prob_ref),
                (mask_hbm, mask_ref),
                (gain_hbm, gain_ref),
                (target_hbm, target_ref),
                (kvw_hbm, kvw),
                (gate_hbm, gate),
                (up_hbm, up),
                (down_hbm, down),
            ]
        )
    ]
    for load in loads:
        load.start()

    def expert_at(group, mid, low):
        return group * 4 + mid * 2 + low

    barrier = pltpu.get_barrier_semaphore()
    for step in range(1, expert_count):
        pl.semaphore_signal(
            barrier,
            inc=1,
            device_id=(me_dp, lax.rem(me + step, expert_count)),
            device_id_type=pl.DeviceIdType.MESH,
        )
    for step in range(1, dp_count):
        pl.semaphore_signal(
            barrier,
            inc=1,
            device_id=(lax.rem(me_dp + step, dp_count), me),
            device_id_type=pl.DeviceIdType.MESH,
        )

    def send(name, number, src, dst, target):
        pltpu.make_async_remote_copy(
            src_ref=src,
            dst_ref=dst,
            send_sem=send_sem.at[send_at[name]],
            recv_sem=recv_sem.at[recv_at[name] + number],
            device_id=target,
            device_id_type=pl.DeviceIdType.MESH,
        ).start()

    def arrived(name, number, like):
        pltpu.make_async_copy(like, like, recv_sem.at[recv_at[name] + number]).wait()

    leaving = []

    def leaves(name, like):
        leaving.append((name, like))

    def to_group(name, step, source, landing, numbered):
        group = swapped(me_group, step)
        for turn in range(1 if step == 0 else 0, 4):
            other = group * 4 + lax.rem(lax.rem(me, 4) + turn, 4)
            send(name, step if numbered else 0, source.at[other], landing, (me_dp, other))

    def dispatch(name, source, landing, work, beside):
        name_x = name + "_x"
        for step in range(groups):
            to_group(name, step, source, landing.at[own_first + me], True)
        landing[own_first + me] = source[me]

        def forward(step):
            count = 3 if step == 0 else 4
            arrived(name, step, landing.at[pl.ds(0, count)])
            span = pl.ds(own_first + swapped(me_group, step) * 4, 4)
            for turn in range(1, dp_count):
                send(name_x, me_dp * groups + step, landing.at[span], landing.at[span], (lax.rem(me_dp + turn, dp_count), me))

        forward(0)
        beside(0)
        for step in range(groups):
            if step + 1 < groups:
                forward(step + 1)
                beside(step + 1)
            for turn in range(1, dp_count):
                other = lax.rem(me_dp + turn, dp_count)
                arrived(name_x, other * groups + step, landing.at[pl.ds(0, 4)])
            work(swapped(me_group, step))
        leaves(name, landing.at[pl.ds(0, expert_count - 1)])
        leaves(name_x, landing.at[pl.ds(0, (dp_count - 1) * expert_count)])

    place_count = expert_count * rows
    older = lax.broadcasted_iota(jnp.int32, (token_rows, token_rows), 0)
    newer = lax.broadcasted_iota(jnp.int32, (token_rows, token_rows), 1)
    before = (older < newer).astype(f32).astype(bf16)
    same = older == newer

    loads[0].wait()
    loads[1].wait()
    names = lax.broadcasted_iota(jnp.int32, (expert_count, token_rows), 0)
    picks = [(names == routes_ref[k : k + 1, :]).astype(f32) for k in range(top_count)]
    counts = dot(sum(picks).astype(bf16), before, (1, 0))
    number = lax.broadcasted_iota(jnp.int32, (place_count, token_rows), 0)
    position = []
    for k in range(top_count):
        slot = jnp.sum(picks[k] * counts, axis=0, keepdims=True).astype(jnp.int32)
        position.append(routes_ref[k : k + 1, :] * rows + slot)
    placed, parts = [], []
    for h in range(halves):
        both = jnp.zeros((place_count, token_rows), f32)
        for k in range(top_count):
            at = (h * top_count + k) * token_rows
            chosen = (number == position[k] + h * capacity).astype(f32)
            place[:, at : at + token_rows] = chosen.astype(bf16)
            both = both + chosen
        placed.append(both.astype(bf16))
        parts.append(tokens_ref[:, h * 128 : (h + 1) * 128])
    sent_rows = dot(jnp.concatenate(placed, axis=1), jnp.concatenate(parts, axis=0), (1, 0))
    rows_out[...] = sent_rows.astype(bf16).reshape(expert_count, rows, 128)
    pl.semaphore_wait(barrier, expert_count - 1 + dp_count - 1)

    def column(row):
        return jnp.sum(jnp.where(same, row, 0), axis=1, keepdims=True)

    all_rows = dp_count * rows
    squares = [jnp.zeros((all_rows, 1), f32)]
    sums = [jnp.zeros((all_rows, 2 * units), f32)]
    block_row = lax.rem(lax.broadcasted_iota(jnp.int32, (all_rows, 1), 0), rows)
    in_half = [(block_row >= h * capacity) & (block_row < (h + 1) * capacity) for h in range(halves)]

    for load in loads[2:6]:
        load.wait()

    def up_projections(group):
        if not squares[1:]:
            for load in loads[7:]:
                load.wait()
            squares.append(None)
        sides, weights = [], []
        for i in range(4):
            f = group * 4 + i
            piece = jnp.concatenate([rows_in[b * expert_count + f] for b in range(dp_count)], axis=0).astype(f32)
            squares[0] = squares[0] + jnp.sum(piece * piece, axis=1, keepdims=True)
            for h in range(halves):
                span = pl.ds(pl.multiple_of(f * width + h * 128, 128), 128)
                sides.append(jnp.where(in_half[h], piece * gain_ref[:, span], 0.0).astype(bf16))
            span = pl.ds(pl.multiple_of(f * width, 128), width)
            weights.append(jnp.concatenate([gate[span, :], up[span, :]], axis=1))
        sums[0] = sums[0] + dot(jnp.concatenate(sides, axis=1), jnp.concatenate(weights, axis=0), (1, 0))

    dispatch("rows", rows_out, rows_in, up_projections, lambda step: None)

    row_number = lax.broadcasted_iota(jnp.int32, (rows, 1), 0)
    for b in range(dp_count):
        span = slice(b * rows, (b + 1) * rows)

        def folded(term):
            full = term
            for h in range(1, halves):
                full = full + pltpu.roll(term, rows - h * capacity, 0)
            return jnp.where(row_number < capacity, full, 0.0)

        mean = folded(jnp.broadcast_to(squares[0][span], (rows, units))) / model_width
        scale = lax.rsqrt(mean + eps_norm)
        gate_val = folded(sums[0][span, :units]) * scale
        up_val = folded(sums[0][span, units:]) * scale
        hidden = gate_val / (1.0 + jnp.exp(-gate_val)) * up_val
        for h in range(halves):
            spread = pltpu.roll(hidden, h * capacity, 0) if h else hidden
            hidden_ref[span, h * units : (h + 1) * units] = spread.astype(bf16)

    for step in reversed(range(groups)):
        group = swapped(me_group, step)
        for i in range(4):
            f = group * 4 + i
            spans = [pl.ds(pl.multiple_of(f * width + h * 128, 128), 128) for h in range(halves)]
            weights = jnp.concatenate([down[:, span] for span in spans], axis=0)
            piece = dot(hidden_ref[...], weights, (1, 0)).astype(bf16)
            for b in range(dp_count):
                part_out[b * expert_count + f] = piece[b * rows : (b + 1) * rows]
        for turn in range(1, dp_count):
            other = lax.rem(me_dp + turn, dp_count)
            send(
                "part_x",
                me_dp * groups + step,
                part_out.at[pl.ds(other * expert_count + group * 4, 4)],
                part_x.at[pl.ds(own_first + group * 4, 4)],
                (other, me),
            )

    def column_work():
        gather = []
        for k in range(top_count):
            spot = column(position[k])
            lanes = lax.broadcasted_iota(jnp.int32, (token_rows, place_count), 1)
            gather.append([(lanes == spot + h * capacity).astype(f32).astype(bf16) for h in range(halves)])
        return gather, [column(prob_ref[k : k + 1, :]) for k in range(top_count)]

    gather, prob_column = column_work()
    hidden_t = hidden_ref[...].astype(f32).T.astype(bf16)
    loads[6].wait()
    own_keys = kvw.shape[1] // expert_count
    turned = kvw[...].T
    for g in range(groups):
        for mid in range(2):
            for low in range(2):
                c = expert_at(g, mid, low)
                kvw_t[low, mid, g] = turned[c * own_keys : (c + 1) * own_keys]
    target = target_ref[...].astype(f32).T

    for step in reversed(range(groups)):
        group = swapped(me_group, step)
        total = part_out[pl.ds(own_first + group * 4, 4)].astype(f32)
        for turn in range(1, dp_count):
            other = lax.rem(me_dp + turn, dp_count)
            arrived("part_x", other * groups + step, part_x.at[pl.ds(0, 4)])
            total = total + part_x[pl.ds(other * expert_count + group * 4, 4)].astype(f32)
        part_sum[pl.ds(group * 4, 4)] = total.astype(bf16)
        to_group("part", step, part_sum, part_in.at[me], False)
    leaves("part_x", part_out.at[pl.ds(0, (dp_count - 1) * expert_count)])
    leaves("part", part_in.at[pl.ds(0, expert_count - 1)])
    part_in[me] = part_sum[me]
    arrived("part", 0, part_in.at[pl.ds(0, expert_count - 1)])

    expert_out = part_in[...].reshape(place_count, 128)
    states = []
    for h in range(halves):
        state = tokens_ref[:, h * 128 : (h + 1) * 128].astype(f32)
        for k in range(top_count):
            state = state + prob_column[k] * dot(gather[k][h], expert_out, (1, 0))
        states.append(state)
    state_wide = jnp.concatenate(states, axis=1) if halves > 1 else states[0]
    state = state_wide.astype(bf16)

    def project(low, mid):
        weights = kvw_t[low, mid].reshape(groups * own_keys, width)
        return dot(weights, state, (1, 1)).reshape(groups, own_keys, token_rows)

    sibling = (me_dp, expert_at(me_group, me_mid, 1 - me_low))
    across = (me_dp, expert_at(me_group, 1 - me_mid, me_low))
    for turn, mid in enumerate((1 - me_mid, me_mid)):
        proj_out[turn] = project(1 - me_low, mid).astype(bf16)
        send("proj_core", turn, proj_out.at[turn], proj_core.at[turn], sibling)
    leaves("proj_core", proj_out)
    far, near = project(me_low, 1 - me_mid), project(me_low, me_mid)
    arrived("proj_core", 0, proj_core.at[0])
    mid_out[...] = (far + proj_core[0].astype(f32)).astype(bf16)
    for step in reversed(range(groups)):
        group = swapped(me_group, step)
        send("proj_mid", step, mid_out.at[group], proj_mid.at[group], across)
    leaves("proj_mid", proj_mid)
    arrived("proj_core", 1, proj_core.at[1])
    proj_core[1] = (near + proj_core[1].astype(f32)).astype(bf16)
    state_t[me_dp] = state_wide.T.astype(bf16)
    for turn in range(1, dp_count):
        send("state", 0, state_t.at[me_dp], state_t.at[me_dp], (lax.rem(me_dp + turn, dp_count), me))
    leaves("state", state_t.at[pl.ds(0, dp_count - 1)])
    key_value = None
    for step in reversed(range(groups)):
        group = swapped(me_group, step)
        arrived("proj_mid", step, proj_mid.at[0])
        summed = proj_core[1, group].astype(f32) + proj_mid[group].astype(f32)
        if step:
            last_out[group] = summed.astype(bf16)
            send("proj", 0, last_out.at[group], proj_in.at[me_group], (me_dp, expert_at(group, me_mid, me_low)))
        else:
            proj_in[me_group] = jnp.zeros(proj_in.shape[1:], bf16)
            key_value = summed
    leaves("proj", proj_in.at[pl.ds(0, groups - 1)])
    arrived("proj", 0, proj_in.at[pl.ds(0, groups - 1)])
    key_value = key_value + jnp.sum(proj_in[...].astype(f32), axis=0)
    cot[me] = (mask_ref[...].astype(f32) * (key_value - target) * token_rows ** (-0.5)).astype(bf16)

    for step in range(1, groups):
        other = expert_at(swapped(me_group, step), me_mid, me_low)
        send("cot", step, cot.at[me], cot.at[me], (me_dp, other))
    for step in range(groups):
        if step:
            arrived("cot", step, cot.at[0])
        c = expert_at(swapped(me_group, step), me_mid, me_low)
        send("cot_mid", step, cot.at[c], cot.at[c], across)
        send("cot_core", 0, cot.at[c], cot.at[c], sibling)
    for step in range(groups):
        arrived("cot_mid", step, cot.at[0])
        c = expert_at(swapped(me_group, step), 1 - me_mid, me_low)
        send("cot_core", 0, cot.at[c], cot.at[c], sibling)
    leaves("cot", cot.at[pl.ds(0, groups - 1)])
    leaves("cot_mid", cot.at[pl.ds(0, groups)])
    leaves("cot_core", cot.at[pl.ds(0, 2 * groups)])

    share = expert_count // dp_count
    pairs = share // 2
    swap_bytes = cot_swap.at[pl.ds(0, (dp_count - 1) * pairs)]
    for turn in range(1, dp_count):
        other = lax.rem(me_dp + turn, dp_count)
        for i in range(pairs):
            part = 2 * i + me_low
            send("swap", 0, cot.at[other * share + part], cot_swap.at[me_dp * share + part], (other, me))
    leaves("swap", swap_bytes)
    arrived("cot_core", 0, cot.at[pl.ds(0, 2 * groups)])

    state_grad_t = dot(kvw[...], cot[...].reshape(kvw.shape[1], token_rows), (1, 0))
    pair_grads = [(state_grad_t * prob_ref[k : k + 1, :]).astype(bf16) for k in range(top_count)]
    sides = [pair_grads[k][h * 128 : (h + 1) * 128] for h in range(halves) for k in range(top_count)]
    grads = dot(place[...], jnp.concatenate(sides, axis=1), (1, 1))
    grad_out[...] = grads.astype(bf16).reshape(expert_count, rows, 128)

    columns = kv_grad_ref.shape[1]

    def beside_grads(step):
        if step == 0:
            own = cot[pl.ds(me_dp * share, share)].reshape(columns, token_rows)
            kv_grad_ref[...] = dot(state_t[me_dp], own, (1, 1))
        if step == 1:
            arrived("swap", 0, swap_bytes)
            for turn in range(1, dp_count):
                other = lax.rem(me_dp + turn, dp_count)
                for i in range(pairs):
                    spot = cot_swap.at[other * share + 2 * i + me_low]
                    send("swap_core", 0, spot, spot, sibling)
            leaves("swap_core", swap_bytes)
        if step == groups - 1:
            arrived("state", 0, state_t.at[pl.ds(0, dp_count - 1)])
            arrived("swap_core", 0, swap_bytes)
            for turn in range(1, dp_count):
                other = lax.rem(me_dp + turn, dp_count)
                theirs = cot_swap[pl.ds(other * share, share)].reshape(columns, token_rows)
                kv_grad_ref[...] += dot(state_t[other], theirs, (1, 1))

    def down_gradient(group):
        pieces = []
        for i in range(4):
            f = group * 4 + i
            pieces.append(jnp.concatenate([grad_in[b * expert_count + f] for b in range(dp_count)], axis=0))
        wide = dot(hidden_t, jnp.concatenate(pieces, axis=1), (1, 0)).astype(bf16)
        for i in range(4):
            for h in range(halves):
                span = pl.ds(pl.multiple_of((group * 4 + i) * width + h * 128, 128), 128)
                down_grad_ref[:, span] = wide[h * units : (h + 1) * units, i * 128 : (i + 1) * 128]

    dispatch("grad", grad_out, grad_in, down_gradient, beside_grads)

    for name, like in leaving:
        pltpu.make_async_copy(like, like, send_sem.at[send_at[name]]).wait()


def per_device(
    tokens,
    norm_gain,
    routes,
    route_prob,
    gate_weight,
    up_weight,
    down_weight,
    key_value_weight,
    key_value_target,
    concept_mask,
):
    token_rows, width = tokens.shape
    top_count = routes.shape[1]
    dp_count, expert_count = lax.axis_size("dp"), lax.axis_size("expert")
    device_count = dp_count * expert_count
    capacity, halves, rows = sizes(dp_count, expert_count, token_rows, top_count, width)
    groups = expert_count // 4
    model_width, units = gate_weight.shape[1:]
    keys = key_value_weight.shape[1]
    own_keys = keys // expert_count
    in_vmem = pl.BlockSpec(memory_space=pltpu.VMEM)
    in_any = pl.BlockSpec(memory_space=pl.ANY)
    pieces = pltpu.VMEM((device_count, rows, 128), bf16)
    own_pieces = pltpu.VMEM((expert_count, rows, 128), bf16)
    group_keys = pltpu.VMEM((groups, own_keys, token_rows), bf16)
    core_keys = pltpu.VMEM((2, groups, own_keys, token_rows), bf16)
    all_keys = pltpu.VMEM((expert_count, own_keys, token_rows), bf16)
    plan, recv_count = sem_plan(dp_count, groups)
    given = (
        tokens,
        routes.T,
        route_prob.T,
        concept_mask[None, :],
        norm_gain[None, :],
        key_value_target,
        key_value_weight,
        gate_weight[0],
        up_weight[0],
        down_weight[0],
    )
    down_grad, kv_grad = pl.pallas_call(
        functools.partial(kernel, dp_count, expert_count, top_count),
        out_shape=(
            jax.ShapeDtypeStruct((units, model_width), bf16),
            jax.ShapeDtypeStruct((width, keys // dp_count), f32),
        ),
        in_specs=[in_any] * len(given),
        out_specs=(in_vmem, in_vmem),
        scratch_shapes=[pltpu.VMEM(x.shape, x.dtype) for x in given]
        + [
            pltpu.VMEM((2, 2, groups, own_keys, width), bf16),
            pltpu.VMEM((expert_count * rows, halves * top_count * token_rows), bf16),
            own_pieces,
            pieces,
            pltpu.VMEM((dp_count * rows, halves * units), bf16),
            pieces,
            pieces,
            own_pieces,
            own_pieces,
            core_keys,
            core_keys,
            group_keys,
            group_keys,
            group_keys,
            group_keys,
            all_keys,
            all_keys,
            pltpu.VMEM((dp_count, width, token_rows), bf16),
            own_pieces,
            pieces,
            pltpu.SemaphoreType.DMA((len(given),)),
            pltpu.SemaphoreType.DMA((len(plan),)),
            pltpu.SemaphoreType.DMA((recv_count,)),
        ],
        compiler_params=pltpu.CompilerParams(
            collective_id=0, has_side_effects=True, vmem_limit_bytes=61 * 1024 * 1024 + 256 * 1024
        ),
    )(*given)
    return (down_grad[None], kv_grad)


def solution(mesh):
    placed = (
        P("dp", "expert"),
        P(),
        P("dp", None),
        P("dp", None),
        P("expert", None, "dp"),
        P("expert", None, "dp"),
        P("expert", "dp", None),
        P("expert", None),
        P("dp", "expert"),
        P("dp"),
    )
    return jax.shard_map(
        per_device,
        mesh=mesh,
        in_specs=placed,
        out_specs=(P("expert", "dp", None), P("expert", "dp")),
        check_vma=False,
    )
```

```python
import functools

import jax
import jax.numpy as jnp
from jax import lax
from jax.experimental import pallas as pl
from jax.experimental.pallas import tpu as pltpu
from jax.sharding import PartitionSpec as P

eps_norm = 1e-06
f32, bf16 = jnp.float32, jnp.bfloat16


def dot(a, b, contract):
    return lax.dot_general(a, b, ((contract[:1], contract[1:]), ((), ())), preferred_element_type=f32)


def swapped(index, step):
    bit = 1
    while bit <= step:
        if step & bit:
            index = index + bit - 2 * bit * lax.rem(lax.div(index, bit), 2)
        bit *= 2
    return index


def sizes(dp_count, expert_count, token_rows, top_count, width):
    capacity = 5 * token_rows * top_count // (4 * expert_count)
    halves = width // 128
    return capacity, halves, -(-halves * capacity // 16) * 16


def sem_plan(dp_count, groups):
    plan, at = {}, 0
    for name, count in (
        ("rows", groups),
        ("rows_x", dp_count * groups),
        ("part_x", dp_count * groups),
        ("part", 1),
        ("proj_core", 2),
        ("proj_mid", groups),
        ("proj", 1),
        ("state", 1),
        ("cot", groups),
        ("cot_mid", groups),
        ("cot_core", 1),
        ("swap", 1),
        ("swap_core", 1),
        ("grad", groups),
        ("grad_x", dp_count * groups),
    ):
        plan[name] = at
        at += count
    return plan, at


def kernel(
    dp_count,
    expert_count,
    top_count,
    tokens_hbm,
    routes_hbm,
    prob_hbm,
    mask_hbm,
    gain_hbm,
    target_hbm,
    kvw_hbm,
    gate_hbm,
    up_hbm,
    down_hbm,
    down_grad_ref,
    kv_grad_ref,
    tokens_ref,
    routes_ref,
    prob_ref,
    mask_ref,
    gain_ref,
    target_ref,
    kvw,
    gate,
    up,
    down,
    kvw_t,
    place,
    rows_out,
    rows_in,
    hidden_ref,
    part_out,
    part_x,
    part_sum,
    part_in,
    proj_out,
    proj_core,
    mid_out,
    proj_mid,
    last_out,
    proj_in,
    cot,
    cot_swap,
    state_t,
    grad_out,
    grad_in,
    load_sem,
    send_sem,
    recv_sem,
):
    token_rows, width = tokens_ref.shape
    rows = rows_out.shape[1]
    capacity, halves, rows_again = sizes(dp_count, expert_count, token_rows, top_count, width)
    assert rows == rows_again
    units = gate.shape[1]
    model_width = width * expert_count
    groups = expert_count // 4
    recv_at, _ = sem_plan(dp_count, groups)
    send_at = {name: i for i, name in enumerate(recv_at)}
    me_dp, me = lax.axis_index("dp"), lax.axis_index("expert")
    me_group, me_mid, me_low = lax.div(me, 4), lax.rem(lax.div(me, 2), 2), lax.rem(me, 2)
    own_first = me_dp * expert_count

    loads = [
        pltpu.make_async_copy(src, dst, load_sem.at[i])
        for i, (src, dst) in enumerate(
            [
                (tokens_hbm, tokens_ref),
                (routes_hbm, routes_ref),
                (prob_hbm, prob_ref),
                (mask_hbm, mask_ref),
                (gain_hbm, gain_ref),
                (target_hbm, target_ref),
                (kvw_hbm, kvw),
                (gate_hbm, gate),
                (up_hbm, up),
                (down_hbm, down),
            ]
        )
    ]
    for load in loads:
        load.start()

    def expert_at(group, mid, low):
        return group * 4 + mid * 2 + low

    barrier = pltpu.get_barrier_semaphore()
    for step in range(1, expert_count):
        pl.semaphore_signal(
            barrier,
            inc=1,
            device_id=(me_dp, lax.rem(me + step, expert_count)),
            device_id_type=pl.DeviceIdType.MESH,
        )
    for step in range(1, dp_count):
        pl.semaphore_signal(
            barrier,
            inc=1,
            device_id=(lax.rem(me_dp + step, dp_count), me),
            device_id_type=pl.DeviceIdType.MESH,
        )

    def send(name, number, src, dst, target):
        pltpu.make_async_remote_copy(
            src_ref=src,
            dst_ref=dst,
            send_sem=send_sem.at[send_at[name]],
            recv_sem=recv_sem.at[recv_at[name] + number],
            device_id=target,
            device_id_type=pl.DeviceIdType.MESH,
        ).start()

    def arrived(name, number, like):
        pltpu.make_async_copy(like, like, recv_sem.at[recv_at[name] + number]).wait()

    leaving = []

    def leaves(name, like):
        leaving.append((name, like))

    def to_group(name, step, source, landing, numbered):
        group = swapped(me_group, step)
        for turn in range(1 if step == 0 else 0, 4):
            other = group * 4 + lax.rem(lax.rem(me, 4) + turn, 4)
            send(name, step if numbered else 0, source.at[other], landing, (me_dp, other))

    def dispatch(name, source, landing, work, beside):
        name_x = name + "_x"
        for step in range(groups):
            to_group(name, step, source, landing.at[own_first + me], True)
        landing[own_first + me] = source[me]

        def forward(step):
            count = 3 if step == 0 else 4
            arrived(name, step, landing.at[pl.ds(0, count)])
            span = pl.ds(own_first + swapped(me_group, step) * 4, 4)
            for turn in range(1, dp_count):
                send(name_x, me_dp * groups + step, landing.at[span], landing.at[span], (lax.rem(me_dp + turn, dp_count), me))

        forward(0)
        beside(0)
        for step in range(groups):
            if step + 1 < groups:
                forward(step + 1)
                beside(step + 1)
            for turn in range(1, dp_count):
                other = lax.rem(me_dp + turn, dp_count)
                arrived(name_x, other * groups + step, landing.at[pl.ds(0, 4)])
            work(swapped(me_group, step))
        leaves(name, landing.at[pl.ds(0, expert_count - 1)])
        leaves(name_x, landing.at[pl.ds(0, (dp_count - 1) * expert_count)])

    place_count = expert_count * rows
    older = lax.broadcasted_iota(jnp.int32, (token_rows, token_rows), 0)
    newer = lax.broadcasted_iota(jnp.int32, (token_rows, token_rows), 1)
    before = (older < newer).astype(f32).astype(bf16)
    same = older == newer

    loads[0].wait()
    loads[1].wait()
    names = lax.broadcasted_iota(jnp.int32, (expert_count, token_rows), 0)
    picks = [(names == routes_ref[k : k + 1, :]).astype(f32) for k in range(top_count)]
    counts = dot(sum(picks).astype(bf16), before, (1, 0))
    number = lax.broadcasted_iota(jnp.int32, (place_count, token_rows), 0)
    position = []
    for k in range(top_count):
        slot = jnp.sum(picks[k] * counts, axis=0, keepdims=True).astype(jnp.int32)
        position.append(routes_ref[k : k + 1, :] * rows + slot)
    placed, parts = [], []
    for h in range(halves):
        both = jnp.zeros((place_count, token_rows), f32)
        for k in range(top_count):
            at = (h * top_count + k) * token_rows
            chosen = (number == position[k] + h * capacity).astype(f32)
            place[:, at : at + token_rows] = chosen.astype(bf16)
            both = both + chosen
        placed.append(both.astype(bf16))
        parts.append(tokens_ref[:, h * 128 : (h + 1) * 128])
    sent_rows = dot(jnp.concatenate(placed, axis=1), jnp.concatenate(parts, axis=0), (1, 0))
    rows_out[...] = sent_rows.astype(bf16).reshape(expert_count, rows, 128)
    pl.semaphore_wait(barrier, expert_count - 1 + dp_count - 1)

    def column(row):
        return jnp.sum(jnp.where(same, row, 0), axis=1, keepdims=True)

    all_rows = dp_count * rows
    squares = [jnp.zeros((all_rows, 1), f32)]
    sums = [jnp.zeros((all_rows, 2 * units), f32)]
    block_row = lax.rem(lax.broadcasted_iota(jnp.int32, (all_rows, 1), 0), rows)
    in_half = [(block_row >= h * capacity) & (block_row < (h + 1) * capacity) for h in range(halves)]

    for load in loads[2:6]:
        load.wait()

    def up_projections(group):
        if not squares[1:]:
            for load in loads[7:]:
                load.wait()
            squares.append(None)
        sides, weights = [], []
        for i in range(4):
            f = group * 4 + i
            piece = jnp.concatenate([rows_in[b * expert_count + f] for b in range(dp_count)], axis=0).astype(f32)
            squares[0] = squares[0] + jnp.sum(piece * piece, axis=1, keepdims=True)
            for h in range(halves):
                span = pl.ds(pl.multiple_of(f * width + h * 128, 128), 128)
                sides.append(jnp.where(in_half[h], piece * gain_ref[:, span], 0.0).astype(bf16))
            span = pl.ds(pl.multiple_of(f * width, 128), width)
            weights.append(jnp.concatenate([gate[span, :], up[span, :]], axis=1))
        sums[0] = sums[0] + dot(jnp.concatenate(sides, axis=1), jnp.concatenate(weights, axis=0), (1, 0))

    target_t = []
    own_keys = kvw.shape[1] // expert_count

    def beside_rows(step):
        if step == 0:
            loads[6].wait()
            turned = kvw[...].T
            for g in range(groups):
                for mid in range(2):
                    for low in range(2):
                        c = expert_at(g, mid, low)
                        kvw_t[low, mid, g] = turned[c * own_keys : (c + 1) * own_keys]
            target_t.append(target_ref[...].astype(f32).T)

    dispatch("rows", rows_out, rows_in, up_projections, beside_rows)

    row_number = lax.broadcasted_iota(jnp.int32, (rows, 1), 0)
    for b in range(dp_count):
        span = slice(b * rows, (b + 1) * rows)

        def folded(term):
            full = term
            for h in range(1, halves):
                full = full + pltpu.roll(term, rows - h * capacity, 0)
            return jnp.where(row_number < capacity, full, 0.0)

        mean = folded(jnp.broadcast_to(squares[0][span], (rows, units))) / model_width
        scale = lax.rsqrt(mean + eps_norm)
        gate_val = folded(sums[0][span, :units]) * scale
        up_val = folded(sums[0][span, units:]) * scale
        hidden = gate_val / (1.0 + jnp.exp(-gate_val)) * up_val
        for h in range(halves):
            spread = pltpu.roll(hidden, h * capacity, 0) if h else hidden
            hidden_ref[span, h * units : (h + 1) * units] = spread.astype(bf16)

    for step in reversed(range(groups)):
        group = swapped(me_group, step)
        for i in range(4):
            f = group * 4 + i
            spans = [pl.ds(pl.multiple_of(f * width + h * 128, 128), 128) for h in range(halves)]
            weights = jnp.concatenate([down[:, span] for span in spans], axis=0)
            piece = dot(hidden_ref[...], weights, (1, 0)).astype(bf16)
            for b in range(dp_count):
                part_out[b * expert_count + f] = piece[b * rows : (b + 1) * rows]
        for turn in range(1, dp_count):
            other = lax.rem(me_dp + turn, dp_count)
            send(
                "part_x",
                me_dp * groups + step,
                part_out.at[pl.ds(other * expert_count + group * 4, 4)],
                part_x.at[pl.ds(own_first + group * 4, 4)],
                (other, me),
            )

    def column_work():
        gather = []
        for k in range(top_count):
            spot = column(position[k])
            lanes = lax.broadcasted_iota(jnp.int32, (token_rows, place_count), 1)
            gather.append([(lanes == spot + h * capacity).astype(f32).astype(bf16) for h in range(halves)])
        return gather, [column(prob_ref[k : k + 1, :]) for k in range(top_count)]

    gather, prob_column = column_work()
    hidden_t = hidden_ref[...].astype(f32).T.astype(bf16)
    for step in reversed(range(groups)):
        group = swapped(me_group, step)
        total = part_out[pl.ds(own_first + group * 4, 4)].astype(f32)
        for turn in range(1, dp_count):
            other = lax.rem(me_dp + turn, dp_count)
            arrived("part_x", other * groups + step, part_x.at[pl.ds(0, 4)])
            total = total + part_x[pl.ds(other * expert_count + group * 4, 4)].astype(f32)
        part_sum[pl.ds(group * 4, 4)] = total.astype(bf16)
        to_group("part", step, part_sum, part_in.at[me], False)
    leaves("part_x", part_out.at[pl.ds(0, (dp_count - 1) * expert_count)])
    leaves("part", part_in.at[pl.ds(0, expert_count - 1)])
    part_in[me] = part_sum[me]
    arrived("part", 0, part_in.at[pl.ds(0, expert_count - 1)])

    expert_out = part_in[...].reshape(place_count, 128)
    states = []
    for h in range(halves):
        state = tokens_ref[:, h * 128 : (h + 1) * 128].astype(f32)
        for k in range(top_count):
            state = state + prob_column[k] * dot(gather[k][h], expert_out, (1, 0))
        states.append(state)
    state_wide = jnp.concatenate(states, axis=1) if halves > 1 else states[0]
    state = state_wide.astype(bf16)

    def project(low, mid):
        weights = kvw_t[low, mid].reshape(groups * own_keys, width)
        return dot(weights, state, (1, 1)).reshape(groups, own_keys, token_rows)

    sibling = (me_dp, expert_at(me_group, me_mid, 1 - me_low))
    across = (me_dp, expert_at(me_group, 1 - me_mid, me_low))
    for turn, mid in enumerate((1 - me_mid, me_mid)):
        proj_out[turn] = project(1 - me_low, mid).astype(bf16)
        send("proj_core", turn, proj_out.at[turn], proj_core.at[turn], sibling)
    leaves("proj_core", proj_out)
    far, near = project(me_low, 1 - me_mid), project(me_low, me_mid)
    arrived("proj_core", 0, proj_core.at[0])
    mid_out[...] = (far + proj_core[0].astype(f32)).astype(bf16)
    for step in reversed(range(groups)):
        group = swapped(me_group, step)
        send("proj_mid", step, mid_out.at[group], proj_mid.at[group], across)
    leaves("proj_mid", proj_mid)
    arrived("proj_core", 1, proj_core.at[1])
    proj_core[1] = (near + proj_core[1].astype(f32)).astype(bf16)
    state_t[me_dp] = state_wide.T.astype(bf16)
    for turn in range(1, dp_count):
        send("state", 0, state_t.at[me_dp], state_t.at[me_dp], (lax.rem(me_dp + turn, dp_count), me))
    leaves("state", state_t.at[pl.ds(0, dp_count - 1)])
    key_value = None
    for step in reversed(range(groups)):
        group = swapped(me_group, step)
        arrived("proj_mid", step, proj_mid.at[0])
        summed = proj_core[1, group].astype(f32) + proj_mid[group].astype(f32)
        if step:
            last_out[group] = summed.astype(bf16)
            send("proj", 0, last_out.at[group], proj_in.at[me_group], (me_dp, expert_at(group, me_mid, me_low)))
        else:
            proj_in[me_group] = jnp.zeros(proj_in.shape[1:], bf16)
            key_value = summed
    leaves("proj", proj_in.at[pl.ds(0, groups - 1)])
    arrived("proj", 0, proj_in.at[pl.ds(0, groups - 1)])
    key_value = key_value + jnp.sum(proj_in[...].astype(f32), axis=0)
    cot[me] = (mask_ref[...].astype(f32) * (key_value - target_t[0]) * token_rows ** (-0.5)).astype(bf16)

    for step in range(1, groups):
        other = expert_at(swapped(me_group, step), me_mid, me_low)
        send("cot", step, cot.at[me], cot.at[me], (me_dp, other))
    for step in range(groups):
        if step:
            arrived("cot", step, cot.at[0])
        c = expert_at(swapped(me_group, step), me_mid, me_low)
        send("cot_mid", step, cot.at[c], cot.at[c], across)
        send("cot_core", 0, cot.at[c], cot.at[c], sibling)
    for step in range(groups):
        arrived("cot_mid", step, cot.at[0])
        c = expert_at(swapped(me_group, step), 1 - me_mid, me_low)
        send("cot_core", 0, cot.at[c], cot.at[c], sibling)
    leaves("cot", cot.at[pl.ds(0, groups - 1)])
    leaves("cot_mid", cot.at[pl.ds(0, groups)])
    leaves("cot_core", cot.at[pl.ds(0, 2 * groups)])

    share = expert_count // dp_count
    pairs = share // 2
    swap_bytes = cot_swap.at[pl.ds(0, (dp_count - 1) * pairs)]
    for turn in range(1, dp_count):
        other = lax.rem(me_dp + turn, dp_count)
        for i in range(pairs):
            part = 2 * i + me_low
            send("swap", 0, cot.at[other * share + part], cot_swap.at[me_dp * share + part], (other, me))
    leaves("swap", swap_bytes)
    arrived("cot_core", 0, cot.at[pl.ds(0, 2 * groups)])

    state_grad_t = dot(kvw[...], cot[...].reshape(kvw.shape[1], token_rows), (1, 0))
    pair_grads = [(state_grad_t * prob_ref[k : k + 1, :]).astype(bf16) for k in range(top_count)]
    sides = [pair_grads[k][h * 128 : (h + 1) * 128] for h in range(halves) for k in range(top_count)]
    grads = dot(place[...], jnp.concatenate(sides, axis=1), (1, 1))
    grad_out[...] = grads.astype(bf16).reshape(expert_count, rows, 128)

    columns = kv_grad_ref.shape[1]

    def beside_grads(step):
        if step == 0:
            own = cot[pl.ds(me_dp * share, share)].reshape(columns, token_rows)
            kv_grad_ref[...] = dot(state_t[me_dp], own, (1, 1))
        if step == 1:
            arrived("swap", 0, swap_bytes)
            for turn in range(1, dp_count):
                other = lax.rem(me_dp + turn, dp_count)
                for i in range(pairs):
                    spot = cot_swap.at[other * share + 2 * i + me_low]
                    send("swap_core", 0, spot, spot, sibling)
            leaves("swap_core", swap_bytes)
        if step == groups - 1:
            arrived("state", 0, state_t.at[pl.ds(0, dp_count - 1)])
            arrived("swap_core", 0, swap_bytes)
            for turn in range(1, dp_count):
                other = lax.rem(me_dp + turn, dp_count)
                theirs = cot_swap[pl.ds(other * share, share)].reshape(columns, token_rows)
                kv_grad_ref[...] += dot(state_t[other], theirs, (1, 1))

    def down_gradient(group):
        pieces = []
        for i in range(4):
            f = group * 4 + i
            pieces.append(jnp.concatenate([grad_in[b * expert_count + f] for b in range(dp_count)], axis=0))
        wide = dot(hidden_t, jnp.concatenate(pieces, axis=1), (1, 0)).astype(bf16)
        for i in range(4):
            for h in range(halves):
                span = pl.ds(pl.multiple_of((group * 4 + i) * width + h * 128, 128), 128)
                down_grad_ref[:, span] = wide[h * units : (h + 1) * units, i * 128 : (i + 1) * 128]

    dispatch("grad", grad_out, grad_in, down_gradient, beside_grads)

    for name, like in leaving:
        pltpu.make_async_copy(like, like, send_sem.at[send_at[name]]).wait()


def per_device(
    tokens,
    norm_gain,
    routes,
    route_prob,
    gate_weight,
    up_weight,
    down_weight,
    key_value_weight,
    key_value_target,
    concept_mask,
):
    token_rows, width = tokens.shape
    top_count = routes.shape[1]
    dp_count, expert_count = lax.axis_size("dp"), lax.axis_size("expert")
    device_count = dp_count * expert_count
    capacity, halves, rows = sizes(dp_count, expert_count, token_rows, top_count, width)
    groups = expert_count // 4
    model_width, units = gate_weight.shape[1:]
    keys = key_value_weight.shape[1]
    own_keys = keys // expert_count
    in_vmem = pl.BlockSpec(memory_space=pltpu.VMEM)
    in_any = pl.BlockSpec(memory_space=pl.ANY)
    pieces = pltpu.VMEM((device_count, rows, 128), bf16)
    own_pieces = pltpu.VMEM((expert_count, rows, 128), bf16)
    group_keys = pltpu.VMEM((groups, own_keys, token_rows), bf16)
    core_keys = pltpu.VMEM((2, groups, own_keys, token_rows), bf16)
    all_keys = pltpu.VMEM((expert_count, own_keys, token_rows), bf16)
    plan, recv_count = sem_plan(dp_count, groups)
    given = (
        tokens,
        routes.T,
        route_prob.T,
        concept_mask[None, :],
        norm_gain[None, :],
        key_value_target,
        key_value_weight,
        gate_weight[0],
        up_weight[0],
        down_weight[0],
    )
    down_grad, kv_grad = pl.pallas_call(
        functools.partial(kernel, dp_count, expert_count, top_count),
        out_shape=(
            jax.ShapeDtypeStruct((units, model_width), bf16),
            jax.ShapeDtypeStruct((width, keys // dp_count), f32),
        ),
        in_specs=[in_any] * len(given),
        out_specs=(in_vmem, in_vmem),
        scratch_shapes=[pltpu.VMEM(x.shape, x.dtype) for x in given]
        + [
            pltpu.VMEM((2, 2, groups, own_keys, width), bf16),
            pltpu.VMEM((expert_count * rows, halves * top_count * token_rows), bf16),
            own_pieces,
            pieces,
            pltpu.VMEM((dp_count * rows, halves * units), bf16),
            pieces,
            pieces,
            own_pieces,
            own_pieces,
            core_keys,
            core_keys,
            group_keys,
            group_keys,
            group_keys,
            group_keys,
            all_keys,
            all_keys,
            pltpu.VMEM((dp_count, width, token_rows), bf16),
            own_pieces,
            pieces,
            pltpu.SemaphoreType.DMA((len(given),)),
            pltpu.SemaphoreType.DMA((len(plan),)),
            pltpu.SemaphoreType.DMA((recv_count,)),
        ],
        compiler_params=pltpu.CompilerParams(
            collective_id=0, has_side_effects=True, vmem_limit_bytes=61 * 1024 * 1024 + 256 * 1024
        ),
    )(*given)
    return (down_grad[None], kv_grad)


def solution(mesh):
    placed = (
        P("dp", "expert"),
        P(),
        P("dp", None),
        P("dp", None),
        P("expert", None, "dp"),
        P("expert", None, "dp"),
        P("expert", "dp", None),
        P("expert", None),
        P("dp", "expert"),
        P("dp"),
    )
    return jax.shard_map(
        per_device,
        mesh=mesh,
        in_specs=placed,
        out_specs=(P("expert", "dp", None), P("expert", "dp")),
        check_vma=False,
    )
```
